256 devices in a mesh: lat: 4 (over x_hi, core), lon: 16 (over z, x_lo), rep: 4 (over y).
Axes of the slice: x: 4 (x_hi: 2, x_lo: 2; x = x_hi * 2 + x_lo), y: 4, z: 8, core: 2. Of those that a mesh axis runs over, the one named last changes fastest.
Arguments:
- tokens: bfloat16 [4, 48, 192, 1024], P('rep', 'lat', 'lon'), may hold values from -6 to 6
- grad_out: bfloat16 [4, 48, 192, 1024], P('rep', 'lat', 'lon'), may hold values from -6 to 6
- first_gain: float32 [1024], replicated, may hold values from 0.5 to 1.5
- first_qkv_weight: bfloat16 [1024, 3072], P(('lat', 'lon')), may hold values from -0.1875 to 0.1875
- first_out_weight: bfloat16 [1024, 1024], P(('lat', 'lon')), may hold values from -0.1875 to 0.1875
- first_bias: float32 [529, 16], replicated, may hold values from -300 to 300
- second_gain: float32 [1024], replicated, may hold values from 0.5 to 1.5
- second_qkv_weight: bfloat16 [1024, 3072], P(('lat', 'lon')), may hold values from -0.1875 to 0.1875
- second_out_weight: bfloat16 [1024, 1024], P(('lat', 'lon')), may hold values from -0.1875 to 0.1875
- second_bias: float32 [529, 16], replicated, may hold values from -300 to 300
- rel_index: int32 [144, 144], replicated, may hold values from 0 to 528, as said below
- classes: int32 [48, 192], P('lat', 'lon'), may hold values from 0 to 3, as said below
Outputs:
- token_grad: bfloat16 [4, 48, 192, 1024], P('rep', 'lat', 'lon')
- first_out_grad: float32 [1024, 1024], P(('lat', 'lon'))
- second_out_grad: float32 [1024, 1024], P(('lat', 'lon'))
The draws below stay inside these ranges and needn't reach their ends.
Inputs may be any that keep to these rules, and one draw needn't show every extreme that they name: rel_index[i, j] depends only on the offset between window positions i and j, and distinct offsets name distinct table entries. `classes`: tokens in the last 6 latitude rows of the shifted grid, which came round from the other pole, have class 2 or 3; all others 0 or 1.
All inputs are finite; a program needn't handle non-finite values.
Results may differ from the reference program's by a relative error of at most 0.022.
Values may be sent and summed in bfloat16 or wider, within the bound.
A program may use at most 128 MiB of HBM per device.

```python
import jax
import jax.numpy as jnp
from jax import lax

D = 1024
HEADS = 16
WIN = 12
SHIFT = 6
REL = 529
NLAT = 48
NLON = 192
BATCH = 4


def draw_first_bias(key, part):
    key = jax.random.fold_in(key, 21)
    base = jnp.clip(jax.random.normal(key, (REL, HEADS), jnp.float32), -6.0, 6.0)
    return base


def draw_second_bias(key, part):
    key = jax.random.fold_in(key, 22)
    base = jnp.clip(jax.random.normal(key, (REL, HEADS), jnp.float32), -6.0, 6.0)
    return base


def draw_rel_index(key, part):
    key = jax.random.fold_in(key, 11)
    entries = jax.random.permutation(key, (2 * WIN - 1) ** 2).astype(jnp.int32)
    places = jnp.arange(WIN * WIN, dtype=jnp.int32)
    row_of = places // WIN
    col_of = places % WIN
    offset = (row_of[:, None] - row_of[None, :] + WIN - 1) * (2 * WIN - 1) + (col_of[:, None] - col_of[None, :] + WIN - 1)
    return entries[offset].astype(jnp.int32)


def draw_classes(key, part):
    key = jax.random.fold_in(key, 7)
    surface = jax.random.randint(key, (NLAT, NLON), 0, 2).astype(jnp.int32)
    latitude = lax.broadcasted_iota(jnp.int32, (NLAT, NLON), 0)
    wrapped = (latitude >= NLAT - WIN // 2).astype(jnp.int32)
    return surface + 2 * wrapped


def level_of(own_key, extent, cuts, low, high):
    def one(axis_at, shards_of):
        draws = jax.random.uniform(jax.random.fold_in(jax.random.fold_in(own_key, 6), axis_at), (shards_of,), jnp.float32, low / len(cuts), high / len(cuts))
        return jnp.repeat(jnp.exp(draws), extent[axis_at] // shards_of).reshape((-1,) + (1,) * (len(extent) - axis_at - 1))

    level = one(*cuts[0])
    for cut in cuts[1:]:
        level = level * one(*cut)
    return level


def noise(own_key, shape, scale, most, cuts=(), kind=jnp.bfloat16):
    values = scale * jax.random.normal(own_key, shape, jnp.float32)
    if cuts:
        values = values * level_of(own_key, shape, cuts, -0.22, 0.18)
    return jnp.clip(values, -most, most).astype(kind)


def setup_inputs(seed: int = 0) -> dict:
    keys = jax.random.split(jax.random.key(seed), 13)
    return {
        "tokens": noise(keys[0], (BATCH, NLAT, NLON, D), 1.0, 6.0, ((0, 4), (1, 4), (2, 16))),
        "grad_out": noise(keys[1], (BATCH, NLAT, NLON, D), 1.0, 6.0, ((0, 4), (1, 4), (2, 16))),
        "first_gain": jnp.clip(1.0 + 0.1 * jax.random.normal(keys[2], (D,), jnp.float32), 0.5, 1.5),
        "first_qkv_weight": noise(keys[3], (D, 3 * D), D ** -0.5, 0.1875, ((0, 64),)),
        "first_out_weight": noise(keys[4], (D, D), D ** -0.5, 0.1875, ((0, 64),)),
        "first_bias": draw_first_bias(jax.random.fold_in(keys[12], 71), 0),
        "second_gain": jnp.clip(1.0 + 0.1 * jax.random.normal(keys[6], (D,), jnp.float32), 0.5, 1.5),
        "second_qkv_weight": noise(keys[7], (D, 3 * D), D ** -0.5, 0.1875, ((0, 64),)),
        "second_out_weight": noise(keys[8], (D, D), D ** -0.5, 0.1875, ((0, 64),)),
        "second_bias": draw_second_bias(jax.random.fold_in(keys[12], 71), 0),
        "rel_index": draw_rel_index(jax.random.fold_in(keys[12], 71), 0),
        "classes": draw_classes(jax.random.fold_in(keys[12], 71), 0),
    }


EPSILON = 1e-05

def layer_norm(inputs, gains):
    values = inputs.astype(jnp.float32)
    centered = values - lax.optimization_barrier(jnp.mean(values, axis=-1, keepdims=True))
    spread = lax.optimization_barrier(jnp.mean(centered * centered, axis=-1, keepdims=True))
    return (centered * lax.rsqrt(spread + EPSILON) * gains).astype(jnp.bfloat16)

def to_windows(tensor):
    leading, height, breadth, features = tensor.shape
    blocks = tensor.reshape(leading, height // WIN, WIN, breadth // WIN, WIN, features)
    return blocks.transpose(0, 1, 3, 2, 4, 5).reshape(-1, WIN * WIN, features)

def from_windows(blocks, leading, height, breadth):
    features = blocks.shape[-1]
    tensor = blocks.reshape(leading, height // WIN, breadth // WIN, WIN, WIN, features)
    return tensor.transpose(0, 1, 3, 2, 4, 5).reshape(leading, height, breadth, features)

def window_attention(projected, bias_table, rel_index, classes):
    leading, height, breadth, triple = projected.shape
    features = triple // 3
    head_dim = features // HEADS
    blocks = to_windows(projected)
    windows, positions = (blocks.shape[0], blocks.shape[1])
    pieces = blocks.reshape(windows, positions, 3, HEADS, head_dim).astype(jnp.float32)
    query_part, key_part, value_part = (pieces[:, :, 0], pieces[:, :, 1], pieces[:, :, 2])
    scores = jnp.einsum('wqhc,wkhc->whqk', query_part, key_part) * head_dim ** (-0.5)
    scores = scores + jnp.transpose(bias_table)[:, rel_index][None]
    if classes is not None:
        spread_classes = jnp.broadcast_to(classes[None, :, :, None], (leading, height, breadth, 1))
        labels = to_windows(spread_classes)[:, :, 0]
        matching = labels[:, :, None] == labels[:, None, :]
        scores = jnp.where(matching[:, None], scores, -jnp.inf)
    weights = jax.nn.softmax(scores, axis=-1).astype(jnp.bfloat16)
    mixed = jnp.einsum('whqk,wkhc->wqhc', weights.astype(jnp.float32), value_part).astype(jnp.bfloat16)
    return from_windows(mixed.reshape(windows, positions, features), leading, height, breadth)

def block_forward(inputs, gains, qkv_weight, bias_table, rel_index, classes):
    leading, height, breadth, features = inputs.shape
    normed, norm_pull = jax.vjp(lambda data: layer_norm(data, gains), inputs)
    projected = jnp.dot(normed.reshape(-1, features), qkv_weight, preferred_element_type=jnp.float32).astype(jnp.bfloat16)
    projected = projected.reshape(leading, height, breadth, 3 * features)
    attended, attend_pull = jax.vjp(lambda data: window_attention(data, bias_table, rel_index, classes), projected)
    return (attended, norm_pull, attend_pull)

def block_backward(upstream, attended, norm_pull, attend_pull, qkv_weight, out_weight):
    leading, height, breadth, features = upstream.shape
    flat_up = upstream.reshape(-1, features)
    out_term = jnp.dot(attended.reshape(-1, features).T, flat_up, preferred_element_type=jnp.float32)
    att_grad = jnp.dot(flat_up, out_weight.T, preferred_element_type=jnp.float32).astype(jnp.bfloat16)
    proj_grad, = attend_pull(att_grad.reshape(leading, height, breadth, features))
    normed_grad = jnp.dot(proj_grad.reshape(-1, 3 * features), qkv_weight.T, preferred_element_type=jnp.float32).astype(jnp.bfloat16)
    input_grad, = norm_pull(normed_grad.reshape(leading, height, breadth, features))
    return (input_grad, out_term)

def reference(tokens, grad_out, first_gain, first_qkv_weight, first_out_weight, first_bias, second_gain, second_qkv_weight, second_out_weight, second_bias, rel_index, classes):
    features = tokens.shape[-1]
    first_att, first_norm_pull, first_att_pull = block_forward(tokens, first_gain, first_qkv_weight, first_bias, rel_index, None)
    update = jnp.dot(first_att.reshape(-1, features), first_out_weight, preferred_element_type=jnp.float32).reshape(tokens.shape)
    middle = (tokens.astype(jnp.float32) + update).astype(jnp.bfloat16)
    shifted = jnp.roll(middle, (-SHIFT, -SHIFT), axis=(1, 2))
    shifted_grad = jnp.roll(grad_out, (-SHIFT, -SHIFT), axis=(1, 2))
    second_att, second_norm_pull, second_att_pull = block_forward(shifted, second_gain, second_qkv_weight, second_bias, rel_index, classes)
    second_field_grad, second_term = block_backward(shifted_grad, second_att, second_norm_pull, second_att_pull, second_qkv_weight, second_out_weight)
    returned = jnp.roll(second_field_grad, (SHIFT, SHIFT), axis=(1, 2))
    middle_grad = (grad_out.astype(jnp.float32) + returned.astype(jnp.float32)).astype(jnp.bfloat16)
    first_field_grad, first_term = block_backward(middle_grad, first_att, first_norm_pull, first_att_pull, first_qkv_weight, first_out_weight)
    token_grad = (middle_grad.astype(jnp.float32) + first_field_grad.astype(jnp.float32)).astype(jnp.bfloat16)
    return (token_grad, first_term, second_term)
```

```python
import jax
import jax.numpy as jnp
from jax import lax
from jax.experimental import pallas as pl
from jax.experimental.pallas import tpu as pltpu
from jax.sharding import PartitionSpec as P

HEADS = 16
WIN = 12
HALF = WIN // 2
TOK = WIN * WIN
QUARTER = HALF * HALF
D = 1024
EPSILON = 1e-05
NX, NY, NZ = 4, 4, 8
TABLE = 640
BLOCK = 256
LOW = -1e30
MESH = pl.DeviceIdType.MESH
F32 = jnp.float32
BF16 = jnp.bfloat16

ORDERS = ("zx", "xz", "zx", "xz", "zx", "xz", "zx", "zx")
STARTS = (0, 0, 0, 1, 3, 3, 3, 4)
STAGES = 8


def dot(a, b):
    return jnp.dot(a, b, preferred_element_type=F32)


def dot_t(a, b):
    return lax.dot_general(a, b, (((1,), (1,)), ((), ())), preferred_element_type=F32)


def t_dot(a, b):
    return lax.dot_general(a, b, (((0,), (0,)), ((), ())), preferred_element_type=F32)


def iota(shape, dim):
    return lax.broadcasted_iota(jnp.int32, shape, dim)


def over_six(n):
    return (n * 10923) >> 16


def norm_parts(x):
    centered = x - jnp.mean(x, axis=-1, keepdims=True)
    scale = lax.rsqrt(jnp.mean(centered * centered, axis=-1, keepdims=True) + EPSILON)
    return centered * scale, scale


def norm_back(x, gain, grad):
    unit, scale = norm_parts(x)
    g = grad * gain
    return scale * (
        g - jnp.mean(g, axis=-1, keepdims=True) - unit * jnp.mean(g * unit, axis=-1, keepdims=True)
    )


def kernel(
    tokens_ref, grad_ref, gain1_ref, gain2_ref, wq1_ref, wo1_ref, wq2_ref, wo2_ref,
    tab_ref, rel_ref, cls_ref,
    out_ref, og1_ref, og2_ref,
    wbuf, bias, idx_u, u_raw, u_ref, same, probs, qkv, dqkv, norm_buf, datt,
    tok_f, go_f, mid_f, sh_f, tmp_f, g_stack, att_stack, roll_s, roll_r,
    xs, xr, zs, zr, ys,
    w_local, w_send, w_recv, roll_send, roll_recv, sib_send, sib_recv,
    x_send, x_recv, z_send, z_recv, y_send, y_recv,
):
    lat, lon, y = lax.axis_index("lat"), lax.axis_index("lon"), lax.axis_index("rep")
    xh, core = lat // 2, lat % 2
    z, xl = lon // 2, lon % 2
    x = xh * 2 + xl
    other = 1 - core

    def at_x(d):
        n = (x + d) % NX
        return ((n // 2) * 2 + core, z * 2 + n % 2, y)

    def at_z(d):
        return (lat, ((z + d) % NZ) * 2 + xl, y)

    def at_y(d):
        return (lat, lon, (y + d) % NY)

    sibling = (xh * 2 + other, lon, y)

    def at_roll(a, b):
        return ((lat + a + 4) % 4, (lon + b + 16) % 16, y)

    def copy(src, dst, send, recv, device):
        return pltpu.make_async_remote_copy(
            src_ref=src, dst_ref=dst, send_sem=send, recv_sem=recv,
            device_id=device, device_id_type=MESH,
        )

    local = []
    for u in range(8):
        source = (wq1_ref, wo1_ref, wq2_ref, wo2_ref)[(u // 4) * 2 + (u % 4) // 3]
        column = (u % 4) * D if u % 4 < 3 else 0
        local.append(
            pltpu.make_async_copy(
                source.at[:, pl.ds(column, D)], wbuf.at[u, xh, core, z, xl], w_local.at[u]
            )
        )
        local[-1].start()

    barrier = pltpu.get_barrier_semaphore()
    partners = [at_z(d) for d in range(1, NZ)] + [at_x(d) for d in range(1, NX)]
    partners += [at_y(d) for d in range(1, NY)] + [sibling]
    partners += [at_roll(*s) for s in ((1, 0), (-1, 0), (0, 1), (0, -1), (1, 1), (-1, -1))]
    for partner in partners:
        pl.semaphore_signal(barrier, inc=1, device_id=partner, device_id_type=MESH)
    pl.semaphore_wait(barrier, len(partners))
    for c in local:
        c.wait()

    flights = {}

    def send(u, k, name, src, dst_device):
        c = copy(src, src, w_send.at[u, k], w_recv.at[u, k], dst_device)
        c.start()
        flights[u, name] = c

    def got(u, name):
        flights[u, name].wait_recv()

    def element(u, nx, nz):
        nx = (nx + NX) % NX
        return wbuf.at[u, nx // 2, core, (nz + NZ) % NZ, nx % 2]

    def column(u, nx, first, count):
        nx = (nx + NX) % NX
        return wbuf.at[u, nx // 2, core, pl.ds(first, count), nx % 2]

    def part(u, nx, first):
        nx = (nx + NX) % NX
        return wbuf.at[u, nx // 2, core, z, nx % 2, :, pl.ds(first, 512)]

    def group(u, nz):
        return wbuf.at[u, :, core, (nz + NZ) % NZ]

    def ring_z(u, piece, stage):
        far_right = u % 2 == 0
        if stage > 0:
            if stage < 4 or far_right:
                got(u, f"r{stage}")
            if stage < 4 or not far_right:
                got(u, f"l{stage}")
        if stage < 3 or (stage == 3 and far_right):
            send(u, stage, f"r{stage + 1}", piece(u, z - stage), at_z(1))
        if stage < 3 or (stage == 3 and not far_right):
            send(u, 4 + stage if stage < 3 else 3, f"l{stage + 1}", piece(u, z + stage), at_z(-1 + NZ))

    def share(u):
        send(u, 11, "s", wbuf.at[u, :, core], sibling)

    def gather_stage(u, stage):
        if stage < 0 or stage >= STAGES:
            return
        if ORDERS[u] == "zx":
            if stage <= 4:
                ring_z(u, lambda u, n: element(u, x, n), stage)
            if stage == 4:
                send(u, 7, "xr1", column(u, x, 0, NZ), at_x(1))
                send(u, 8, "xl1", column(u, x, 0, NZ), at_x(3))
            if stage == 5:
                got(u, "xr1")
                send(u, 9, "xr2", column(u, x - 1, 0, 4), at_x(1))
                got(u, "xl1")
                send(u, 10, "xl2", column(u, x + 1, 4, 4), at_x(3))
            if stage == 6:
                got(u, "xr2")
                got(u, "xl2")
                share(u)
        else:
            if stage == 0:
                send(u, 7, "xr1", element(u, x, z), at_x(1))
                send(u, 8, "xl1", element(u, x, z), at_x(3))
            if stage == 1:
                got(u, "xr1")
                send(u, 9, "xr2", part(u, x - 1, 0), at_x(1))
                got(u, "xl1")
                send(u, 10, "xl2", part(u, x + 1, 512), at_x(3))
            if stage == 2:
                got(u, "xr2")
                got(u, "xl2")
            if 2 <= stage <= 6:
                ring_z(u, group, stage - 2)
            if stage == 6:
                share(u)
        if stage == 7:
            got(u, "s")

    clock = [0]

    def gather_turn():
        for u in range(8):
            gather_stage(u, clock[0] - STARTS[u])
        clock[0] += 1

    def gather_until(units):
        while clock[0] < max(STARTS[u] for u in units) + STAGES:
            gather_turn()

    gather_turn()

    for r in range(WIN):
        for source, target in ((tokens_ref, tok_f), (grad_ref, go_f)):
            rows = source[0, r].astype(F32)
            target[pl.ds(r * HALF, HALF), :] = rows[:HALF]
            target[pl.ds(72 + r * HALF, HALF), :] = rows[HALF:]

    rolls = {}

    def roll_out(which, source, back):
        to = 1 if back else -1
        places = ((1, (to, 0)), (2, (0, to)), (3, (to, to))) if back else (
            (2, (to, 0)), (1, (0, to)), (0, (to, to)))
        for i, (quarter, shift) in enumerate(places):
            roll_s[which, i, pl.ds(0, QUARTER), :] = source[
                pl.ds(quarter * QUARTER, QUARTER), :].astype(BF16)
            c = copy(roll_s.at[which, i], roll_r.at[which, i],
                     roll_send.at[which, i], roll_recv.at[which, i], at_roll(*shift))
            c.start()
            rolls[which, i] = c

    def roll_in(which, i):
        rolls[which, i].wait_recv()
        return roll_r[which, i, pl.ds(0, QUARTER), :].astype(F32)

    for which in range(3):
        for i in range(3):
            roll_s[which, i, pl.ds(32, 16), :] = jnp.zeros((16, D), BF16)
    roll_out(0, go_f, False)
    gather_turn()

    k_of = iota((TOK, 512), 0)
    lane = iota((TOK, 512), 1)
    side = (lane >= 256).astype(jnp.int32)
    j = lane - side * (256 + 72)
    s = over_six(jnp.maximum(j, 0))
    c = side * HALF + j - s * HALF
    inside = (j >= 0) & (j < 138)
    late = s > 11
    wanted = jnp.where(late, s - 11, s) * WIN + c
    hit = inside & (k_of == wanted)
    pick_a = jnp.where(hit & (s <= 11), 1.0, 0.0).astype(BF16)
    pick_b = jnp.where(hit & late, 1.0, 0.0).astype(BF16)
    high_a = dot((rel_ref[pl.ds(TOK - WIN, WIN), :] >> 4).astype(F32).astype(BF16), pick_a)
    low_a = dot((rel_ref[pl.ds(TOK - WIN, WIN), :] & 15).astype(F32).astype(BF16), pick_a)
    high_b = dot((rel_ref[pl.ds(0, WIN), :] >> 4).astype(F32).astype(BF16), pick_b)
    low_b = dot((rel_ref[pl.ds(0, WIN), :] & 15).astype(F32).astype(BF16), pick_b)
    idx_u[pl.ds(0, WIN), :] = ((high_a + high_b) * 16.0 + low_a + low_b).astype(jnp.int32)
    gather_turn()

    table = tab_ref[...]
    t_high = table.astype(BF16)
    rest = table - t_high.astype(F32)
    t_mid = rest.astype(BF16)
    t_low = (rest - t_mid.astype(F32)).astype(BF16)
    parts = jnp.concatenate([t_high, t_mid, t_low], axis=0)

    def choose(c1, _):
        chosen = idx_u[pl.ds(c1, 1), :]
        onehot = jnp.where(iota((TABLE, 512), 0) == chosen, 1.0, 0.0).astype(BF16)
        got3 = dot(parts, onehot)
        u_raw[c1] = got3[0:32] + got3[32:64] + got3[64:96]
        return 0

    lax.fori_loop(0, WIN, choose, 0)
    gather_turn()
    for th in range(2 * HEADS):
        rows = u_raw[:, th, :]
        u_ref[th, pl.ds(0, HALF), :] = rows[:HALF]
        u_ref[th, pl.ds(8, HALF), :] = rows[HALF:]

    def slide(th, _):
        left, right = u_ref[th, :, pl.ds(0, 256)], u_ref[th, :, pl.ds(256, 256)]
        first = iota((16, 256), 1) < 72
        for r in range(WIN):
            shift = (256 - HALF * (11 - r)) % 256
            a = pltpu.roll(left, shift, 1) if shift else left
            b = pltpu.roll(right, shift, 1) if shift else right
            value = jnp.where(first, a, b)[:, :TOK]
            bias[th, pl.ds(r * HALF, HALF), :] = value[:HALF]
            bias[th, pl.ds(72 + r * HALF, HALF), :] = value[8:8 + HALF]
        return 0

    lax.fori_loop(0, HEADS, slide, 0)
    gather_turn()

    n = iota((TOK, WIN), 0)
    right_half = (n >= 72).astype(jnp.int32)
    n = n - 72 * right_half
    row_of = over_six(n)
    col_of = right_half * HALF + n - row_of * HALF
    row_pick = jnp.where(iota((TOK, WIN), 1) == row_of, 1.0, 0.0).astype(BF16)
    per_row = dot(row_pick, cls_ref[...].astype(F32).astype(BF16))
    label = jnp.sum(
        jnp.where(iota((TOK, WIN), 1) == col_of, per_row, 0.0), axis=1, keepdims=True)
    member = jnp.where(iota((TOK, 128), 1) == label.astype(jnp.int32), 1.0, 0.0).astype(BF16)
    same[...] = dot_t(member, member)

    lax.fori_loop(HEADS, 2 * HEADS, slide, 0)

    even = jnp.where(iota((1, 128), 1) < 64, 1.0, 0.0).astype(BF16)
    masks = (even, (1.0 - even.astype(F32)).astype(BF16))

    def weight(u, first):
        return wbuf[u, :, :, :, :, :, pl.ds(first, BLOCK)].reshape(D, BLOCK)

    def weight_rows(u, block):
        return wbuf[u, block // 2, block % 2].reshape(BLOCK, D)

    def project(which):
        for u in range(3):
            def step(i, _):
                first = pl.multiple_of(i * BLOCK, BLOCK)
                result = dot(norm_buf[...], weight(which * 4 + u, first))
                qkv[which, :, pl.ds(pl.multiple_of(u * D + first, BLOCK), BLOCK)] = result.astype(BF16)
                return 0
            lax.fori_loop(0, D // BLOCK, step, 0)

    def lanes(i, offset=0):
        return pl.ds(pl.multiple_of(offset + i * 128, 128), 128)

    def attend(which):
        def step(i, _):
            q2 = qkv[which, :, lanes(i)]
            k2 = qkv[which, :, lanes(i, D)]
            v2 = qkv[which, :, lanes(i, 2 * D)]
            mixed = None
            for e in range(2):
                score = dot_t(q2 * masks[e], k2) * 0.125 + bias[which * HEADS + 2 * i + e]
                if which:
                    score = jnp.where(same[...] > 0.5, score, LOW)
                power = jnp.exp(score - jnp.max(score, axis=1, keepdims=True))
                share_of = (power * (1.0 / jnp.sum(power, axis=1, keepdims=True))).astype(BF16)
                probs[which * HEADS + 2 * i + e] = share_of
                term = dot(share_of, v2 * masks[e])
                mixed = term if mixed is None else mixed + term
            att_stack[which, i // 2, pl.ds(0, TOK), lanes(i % 2)] = mixed.astype(BF16)
            return 0
        lax.fori_loop(0, HEADS // 2, step, 0)

    def attend_back(which):
        def step(i, _):
            q2 = qkv[which, :, lanes(i)]
            k2 = qkv[which, :, lanes(i, D)]
            v2 = qkv[which, :, lanes(i, 2 * D)]
            do2 = datt[:, lanes(i)]
            dq = dk = dv = None
            for e in range(2):
                share_of = probs[which * HEADS + 2 * i + e]
                up = do2 * masks[e]
                dp = dot_t(up, v2)
                share_f = share_of.astype(F32)
                mean = jnp.sum(dp * share_f, axis=1, keepdims=True)
                ds = (share_f * (dp - mean) * 0.125).astype(BF16)
                a = t_dot(share_of, up)
                b = dot(ds, k2 * masks[e])
                c = t_dot(ds, q2 * masks[e])
                dv = a if dv is None else dv + a
                dq = b if dq is None else dq + b
                dk = c if dk is None else dk + c
            dqkv[:, lanes(i)] = dq.astype(BF16)
            dqkv[:, lanes(i, D)] = dk.astype(BF16)
            dqkv[:, lanes(i, 2 * D)] = dv.astype(BF16)
            return 0
        lax.fori_loop(0, HEADS // 2, step, 0)

    def att_grad(which):
        for b in range(4):
            datt[:, pl.ds(b * BLOCK, BLOCK)] = dot_t(
                g_stack[which, pl.ds(0, TOK), :], weight_rows(which * 4 + 3, b)).astype(BF16)

    def normed_grad(which):
        for b in range(4):
            result = None
            for u in range(3):
                term = dot_t(dqkv[:, pl.ds(u * D, D)], weight_rows(which * 4 + u, b))
                result = term if result is None else result + term
            tmp_f[:, pl.ds(b * BLOCK, BLOCK)] = result.astype(BF16).astype(F32)

    sibs = {}

    def to_sibling(name, k, src, dst):
        c = copy(src, dst, sib_send.at[k], sib_recv.at[k], sibling)
        c.start()
        sibs[name] = c

    def send_att(m):
        for h in range(2):
            to_sibling((m, h), m * 3 + h, att_stack.at[m, h * 2 + other, pl.ds(0, TOK)],
                       att_stack.at[m, h * 2 + other, pl.ds(TOK, TOK)])

    def send_grad(m):
        to_sibling((m, 2), m * 3 + 2, g_stack.at[m, pl.ds(0, TOK)], g_stack.at[m, pl.ds(TOK, TOK)])

    xflights, zflights, yflights = {}, {}, {}

    def reduce_x(m):
        for k in range(3):
            sibs[m, k].wait_recv()
        for h in range(2):
            def step(i, _):
                cols = pl.ds(pl.multiple_of(i * BLOCK, BLOCK), BLOCK)
                result = t_dot(att_stack[m, h * 2 + core], g_stack[m, :, cols]).astype(BF16)
                xs[m, h, :, :, :, cols] = result.reshape(NZ, 2, 16, BLOCK)
                return 0
            lax.fori_loop(0, D // BLOCK, step, 0)
        for d in (2, 1, 3):
            target = (x + d) % NX
            c = copy(xs.at[m, target // 2, :, target % 2], xr.at[m, d - 1],
                     x_send.at[m, d - 1], x_recv.at[m, d - 1], at_x(d))
            c.start()
            xflights[m, d] = c

    def reduce_z(m):
        for d in range(1, NX):
            xflights[m, d].wait_recv()

        def step(i, _):
            value = xs[m, xh, i, xl].astype(F32)
            for d in range(NX - 1):
                value = value + xr[m, d, i].astype(F32)
            zs[m, i] = value.astype(BF16)
            return 0
        lax.fori_loop(0, NZ, step, 0)
        for d in (4, 3, 5, 2, 6, 1, 7):
            c = copy(zs.at[m, (z + d) % NZ], zr.at[m, d - 1],
                     z_send.at[m, d - 1], z_recv.at[m, d - 1], at_z(d))
            c.start()
            zflights[m, d] = c

    def reduce_y(m):
        for d in range(1, NZ):
            zflights[m, d].wait_recv()
        value = zs[m, z].astype(F32)
        for d in range(NZ - 1):
            value = value + zr[m, d].astype(F32)
        ys[m, y] = value.astype(BF16)
        for d in range(1, NY):
            c = copy(ys.at[m, y], ys.at[m, y], y_send.at[m, d - 1], y_recv.at[m, d - 1], at_y(d))
            c.start()
            yflights[m, d] = c

    def reduce_end(m, target):
        for d in range(1, NY):
            yflights[m, d].wait_recv()
        value = ys[m, 0].astype(F32)
        for i in range(1, NY):
            value = value + ys[m, i].astype(F32)
        target[...] = value

    unit, _ = norm_parts(tok_f[...])
    norm_buf[...] = (unit * gain1_ref[...]).astype(BF16)
    gather_until((0, 1, 2))
    project(0)
    gather_turn()
    attend(0)
    send_att(0)
    gather_until((3,))
    for b in range(4):
        cols = pl.ds(b * BLOCK, BLOCK)
        result = tok_f[:, cols]
        for h in range(4):
            result = result + dot(att_stack[0, h, pl.ds(0, TOK), :],
                                  wbuf[3, h // 2, h % 2, :, :, :, cols].reshape(BLOCK, BLOCK))
        mid_f[:, cols] = result.astype(BF16).astype(F32)
    roll_out(1, mid_f, False)
    sh_f[pl.ds(0, QUARTER), :] = go_f[pl.ds(3 * QUARTER, QUARTER), :]
    for i in range(3):
        sh_f[pl.ds((i + 1) * QUARTER, QUARTER), :] = roll_in(0, i)
    g_stack[1, pl.ds(0, TOK), :] = sh_f[...].astype(BF16)
    send_grad(1)
    gather_until(range(8))
    att_grad(1)
    sh_f[pl.ds(0, QUARTER), :] = mid_f[pl.ds(3 * QUARTER, QUARTER), :]
    for i in range(3):
        sh_f[pl.ds((i + 1) * QUARTER, QUARTER), :] = roll_in(1, i)
    unit, _ = norm_parts(sh_f[...])
    norm_buf[...] = (unit * gain2_ref[...]).astype(BF16)
    project(1)
    attend(1)
    send_att(1)
    attend_back(1)
    reduce_x(1)
    normed_grad(1)
    mid_f[...] = norm_back(sh_f[...], gain2_ref[...], tmp_f[...])
    roll_out(2, mid_f, True)
    sh_f[pl.ds(3 * QUARTER, QUARTER), :] = mid_f[pl.ds(0, QUARTER), :].astype(BF16).astype(F32)
    reduce_z(1)
    for i, quarter in enumerate((2, 1, 0)):
        sh_f[pl.ds(quarter * QUARTER, QUARTER), :] = roll_in(2, i)
    mid_f[...] = (go_f[...] + sh_f[...]).astype(BF16).astype(F32)
    g_stack[0, pl.ds(0, TOK), :] = mid_f[...].astype(BF16)
    send_grad(0)
    att_grad(0)
    reduce_x(0)
    attend_back(0)
    reduce_y(1)
    normed_grad(0)
    reduce_z(0)
    sh_f[...] = mid_f[...] + norm_back(tok_f[...], gain1_ref[...], tmp_f[...]).astype(BF16).astype(F32)
    for r in range(WIN):
        rows = jnp.concatenate(
            [sh_f[pl.ds(r * HALF, HALF), :], sh_f[pl.ds(72 + r * HALF, HALF), :]], axis=0)
        out_ref[0, r] = rows.astype(BF16)
    reduce_end(1, og2_ref)
    reduce_y(0)
    reduce_end(0, og1_ref)
    for group_of in (flights, rolls, sibs, xflights, zflights, yflights):
        for c in group_of.values():
            c.wait_send()


def on_device(
    tokens, grad_out, first_gain, first_qkv_weight, first_out_weight, first_bias,
    second_gain, second_qkv_weight, second_out_weight, second_bias, rel_index, classes,
):
    table = jnp.concatenate([first_bias, second_bias], axis=1).T
    table = jnp.pad(table, ((0, 0), (0, TABLE - table.shape[1])))
    vmem = pl.BlockSpec(memory_space=pltpu.VMEM)
    hbm = pl.BlockSpec(memory_space=pl.ANY)
    dma = pltpu.SemaphoreType.DMA
    return pl.pallas_call(
        kernel,
        out_shape=(
            jax.ShapeDtypeStruct((1, WIN, WIN, D), BF16),
            jax.ShapeDtypeStruct((16, D), F32),
            jax.ShapeDtypeStruct((16, D), F32),
        ),
        in_specs=[vmem] * 4 + [hbm] * 4 + [vmem] * 3,
        out_specs=(vmem, vmem, vmem),
        scratch_shapes=[
            pltpu.VMEM((8, 2, 2, NZ, 2, 16, D), BF16),
            pltpu.VMEM((2 * HEADS, TOK, TOK), F32),
            pltpu.VMEM((16, 512), jnp.int32),
            pltpu.VMEM((WIN, 2 * HEADS, 512), F32),
            pltpu.VMEM((2 * HEADS, 16, 512), F32),
            pltpu.VMEM((TOK, TOK), F32),
            pltpu.VMEM((2 * HEADS, TOK, TOK), BF16),
            pltpu.VMEM((2, TOK, 3 * D), BF16),
            pltpu.VMEM((TOK, 3 * D), BF16),
            pltpu.VMEM((TOK, D), BF16),
            pltpu.VMEM((TOK, D), BF16),
            pltpu.VMEM((TOK, D), F32),
            pltpu.VMEM((TOK, D), F32),
            pltpu.VMEM((TOK, D), F32),
            pltpu.VMEM((TOK, D), F32),
            pltpu.VMEM((TOK, D), F32),
            pltpu.VMEM((2, 2 * TOK, D), BF16),
            pltpu.VMEM((2, 4, 2 * TOK, BLOCK), BF16),
            pltpu.VMEM((3, 3, 48, D), BF16),
            pltpu.VMEM((3, 3, 48, D), BF16),
            pltpu.VMEM((2, 2, NZ, 2, 16, D), BF16),
            pltpu.VMEM((2, NX - 1, NZ, 16, D), BF16),
            pltpu.VMEM((2, NZ, 16, D), BF16),
            pltpu.VMEM((2, NZ - 1, 16, D), BF16),
            pltpu.VMEM((2, NY, 16, D), BF16),
            dma((8,)),
            dma((8, 12)), dma((8, 12)),
            dma((3, 3)), dma((3, 3)),
            dma((6,)), dma((6,)),
            dma((2, NX - 1)), dma((2, NX - 1)),
            dma((2, NZ - 1)), dma((2, NZ - 1)),
            dma((2, NY - 1)), dma((2, NY - 1)),
        ],
        compiler_params=pltpu.CompilerParams(
            collective_id=0, has_side_effects=True, vmem_limit_bytes=56 * 1024 * 1024
        ),
        name="window_blocks",
    )(
        tokens, grad_out, first_gain[None], second_gain[None],
        first_qkv_weight, first_out_weight, second_qkv_weight, second_out_weight,
        table, rel_index, classes,
    )


def solution(mesh):
    tile = P("rep", "lat", "lon", None)
    rows = P(("lat", "lon"), None)
    in_specs = (tile, tile, P(), rows, rows, P(), P(), rows, rows, P(), P(), P("lat", "lon"))
    return jax.shard_map(
        on_device, mesh=mesh, in_specs=in_specs, out_specs=(tile, rows, rows), check_vma=False
    )
```

```python
import jax
import jax.numpy as jnp
from jax import lax
from jax.experimental import pallas as pl
from jax.experimental.pallas import tpu as pltpu
from jax.sharding import PartitionSpec as P

HEADS = 16
WIN = 12
HALF = WIN // 2
TOK = WIN * WIN
QUARTER = HALF * HALF
D = 1024
EPSILON = 1e-05
NX, NY, NZ = 4, 4, 8
TABLE = 640
BLOCK = 256
LOW = -1e30
MESH = pl.DeviceIdType.MESH
F32 = jnp.float32
BF16 = jnp.bfloat16

ORDERS = ("zxy", "zyx", "xyz", "zxy", "zyx", "zxy", "xyz", "zyx")
STARTS = (0, 0, 0, 1, 1, 2, 2, 2)
STAGES = 6


def dot(a, b):
    return jnp.dot(a, b, preferred_element_type=F32)


def dot_t(a, b):
    return lax.dot_general(a, b, (((1,), (1,)), ((), ())), preferred_element_type=F32)


def t_dot(a, b):
    return lax.dot_general(a, b, (((0,), (0,)), ((), ())), preferred_element_type=F32)


def iota(shape, dim):
    return lax.broadcasted_iota(jnp.int32, shape, dim)


def over_six(n):
    return (n * 10923) >> 16


def norm_parts(x):
    centered = x - jnp.mean(x, axis=-1, keepdims=True)
    scale = lax.rsqrt(jnp.mean(centered * centered, axis=-1, keepdims=True) + EPSILON)
    return centered * scale, scale


def norm_back(x, gain, grad):
    unit, scale = norm_parts(x)
    g = grad * gain
    return scale * (
        g - jnp.mean(g, axis=-1, keepdims=True) - unit * jnp.mean(g * unit, axis=-1, keepdims=True)
    )


def kernel(
    tokens_ref, grad_ref, gain1_ref, gain2_ref, wq1_ref, wo1_ref, wq2_ref, wo2_ref,
    tab_ref, rel_ref, cls_ref,
    out_ref, og1_ref, og2_ref,
    wbuf, bias, idx_u, u_raw, u_ref, same, probs, qkv, dqkv, norm_buf, datt,
    tok_f, go_f, mid_f, sh_f, tmp_f, g_stack, att_stack, roll_s, roll_r,
    att_t, early, xs, xr, zs, zr, ys, vs, vr, ws, wr, us, ur, os,
    w_local, w_send, w_recv, roll_send, roll_recv, sib_send, sib_recv, red_send, red_recv,
):
    lat, lon, y = lax.axis_index("lat"), lax.axis_index("lon"), lax.axis_index("rep")
    xh, core = lat // 2, lat % 2
    z, xl = lon // 2, lon % 2
    x = xh * 2 + xl
    other = 1 - core

    def at_x(d):
        n = (x + d) % NX
        return ((n // 2) * 2 + core, z * 2 + n % 2, y)

    def at_z(d):
        return (lat, ((z + d) % NZ) * 2 + xl, y)

    def at_y(d):
        return (lat, lon, (y + d) % NY)

    sibling = (xh * 2 + other, lon, y)

    def at_roll(a, b):
        return ((lat + a + 4) % 4, (lon + b + 16) % 16, y)

    def copy(src, dst, send, recv, device):
        return pltpu.make_async_remote_copy(
            src_ref=src, dst_ref=dst, send_sem=send, recv_sem=recv,
            device_id=device, device_id_type=MESH,
        )

    local = []
    for u in range(8):
        source = (wq1_ref, wo1_ref, wq2_ref, wo2_ref)[(u // 4) * 2 + (u % 4) // 3]
        column = (u % 4) * D if u % 4 < 3 else 0
        local.append(
            pltpu.make_async_copy(
                source.at[:, pl.ds(pl.multiple_of(column + y * BLOCK, BLOCK), BLOCK)],
                wbuf.at[u, y, xh, core, z, xl], w_local.at[u],
            )
        )
        local[-1].start()

    barrier = pltpu.get_barrier_semaphore()
    partners = [at_z(d) for d in range(1, NZ)] + [at_x(d) for d in range(1, NX)]
    partners += [at_y(d) for d in range(1, NY)] + [sibling]
    partners += [at_roll(*s) for s in ((1, 0), (-1, 0), (0, 1), (0, -1), (1, 1), (-1, -1))]
    for partner in partners:
        pl.semaphore_signal(barrier, inc=1, device_id=partner, device_id_type=MESH)
    pl.semaphore_wait(barrier, len(partners))
    for c in local:
        c.wait()

    flights, counts = {}, [0] * 8

    def send(u, tag, src, device):
        k = counts[u]
        counts[u] += 1
        c = copy(src, src, w_send.at[u, k], w_recv.at[u, k], device)
        c.start()
        flights[u, k] = c
        waits.setdefault((u, tag), []).append(c)

    waits = {}

    def got(u, tag):
        for c in waits[u, tag]:
            c.wait_recv()

    def element(u):
        return wbuf.at[u, y, xh, core, z, xl]

    def wrap(n, size):
        return (n + size) % size

    def spread(u, tag, src, at, size):
        for d in sorted(range(1, size), key=lambda d: -min(d, size - d)):
            send(u, tag, src, at(d))

    def share(u, src):
        send(u, "share", src, sibling)

    def stage_zxy(u, stage):
        def plane(d):
            return wbuf.at[u, wrap(y + d, NY), :, core]

        def half(d, h):
            return wbuf.at[u, wrap(y + d, NY), h, core]

        if stage == 0:
            spread(u, 0, element(u), at_z, NZ)
        if stage == 1:
            got(u, 0)
            spread(u, 1, wbuf.at[u, y, xh, core, :, xl], at_x, NX)
        if stage == 2:
            got(u, 1)
            send(u, "r1", half(0, 0), at_y(1))
            send(u, "l1", half(0, 1), at_y(3))
            send(u, "r2", half(0, 1), at_y(1))
            send(u, "l2", half(0, 0), at_y(3))
            share(u, plane(0))
        if stage == 3:
            got(u, "r1")
            send(u, "far", half(-1, 0), at_y(1))
            got(u, "l1")
            send(u, "far", half(1, 1), at_y(3))
            got(u, "r2")
            share(u, plane(-1))
            got(u, "l2")
            share(u, plane(1))
        if stage == 4:
            got(u, "far")
            share(u, plane(2))

    def stage_zyx(u, stage):
        def column(d):
            n = wrap(x + d, NX)
            return wbuf.at[u, :, n // 2, core, :, n % 2]

        def half(d, h):
            n = wrap(x + d, NX)
            return wbuf.at[u, pl.ds(2 * h, 2), n // 2, core, :, n % 2]

        if stage == 0:
            spread(u, 0, element(u), at_z, NZ)
        if stage == 1:
            got(u, 0)
            spread(u, 1, wbuf.at[u, y, xh, core, :, xl], at_y, NY)
        if stage == 2:
            got(u, 1)
            send(u, "r1", half(0, 0), at_x(1))
            send(u, "l1", half(0, 1), at_x(3))
            send(u, "r2", half(0, 1), at_x(1))
            send(u, "l2", half(0, 0), at_x(3))
            share(u, column(0))
        if stage == 3:
            got(u, "r1")
            send(u, "far", half(-1, 0), at_x(1))
            got(u, "l1")
            send(u, "far", half(1, 1), at_x(3))
            got(u, "r2")
            share(u, column(-1))
            got(u, "l2")
            share(u, column(1))
        if stage == 4:
            got(u, "far")
            share(u, column(2))

    def stage_xyz(u, stage):
        def group(d):
            return wbuf.at[u, :, :, core, wrap(z + d, NZ)]

        def half(d, h):
            return wbuf.at[u, pl.ds(2 * h, 2), :, core, wrap(z + d, NZ)]

        if stage == 0:
            spread(u, 0, element(u), at_x, NX)
        if stage == 1:
            got(u, 0)
            spread(u, 1, wbuf.at[u, y, :, core, z], at_y, NY)
        if stage == 2:
            got(u, 1)
            send(u, "r2", group(0), at_z(2))
            send(u, "l2", group(0), at_z(6))
            send(u, "r1", group(0), at_z(1))
            send(u, "l1", group(0), at_z(7))
            share(u, group(0))
        if stage == 3:
            got(u, "r2")
            send(u, "far", half(-2, 0), at_z(2))
            send(u, "far", group(-2), at_z(1))
            got(u, "l2")
            send(u, "far", half(2, 1), at_z(6))
            send(u, "far", group(2), at_z(7))
            got(u, "r1")
            got(u, "l1")
            for d in (-2, -1, 1, 2):
                share(u, group(d))
        if stage == 4:
            got(u, "far")
            for d in (-3, 3, 4):
                share(u, group(d))

    def gather_stage(u, stage):
        if 0 <= stage < STAGES:
            {"zxy": stage_zxy, "zyx": stage_zyx, "xyz": stage_xyz}[ORDERS[u]](u, stage)
        if stage == 5:
            got(u, "share")

    clock = [0]

    def gather_turn():
        for u in range(8):
            gather_stage(u, clock[0] - STARTS[u])
        clock[0] += 1

    def gather_until(units):
        while clock[0] < max(STARTS[u] for u in units) + STAGES:
            gather_turn()

    gather_turn()

    for r in range(WIN):
        for source, target in ((tokens_ref, tok_f), (grad_ref, go_f)):
            rows = source[0, r].astype(F32)
            target[pl.ds(r * HALF, HALF), :] = rows[:HALF]
            target[pl.ds(72 + r * HALF, HALF), :] = rows[HALF:]

    rolls = {}

    def roll_out(which, source, back):
        to = 1 if back else -1
        places = ((1, (to, 0)), (2, (0, to)), (3, (to, to))) if back else (
            (2, (to, 0)), (1, (0, to)), (0, (to, to)))
        for i, (quarter, shift) in enumerate(places):
            roll_s[which, i, pl.ds(0, QUARTER), :] = source[
                pl.ds(quarter * QUARTER, QUARTER), :].astype(BF16)
            c = copy(roll_s.at[which, i], roll_r.at[which, i],
                     roll_send.at[which, i], roll_recv.at[which, i], at_roll(*shift))
            c.start()
            rolls[which, i] = c

    def roll_in(which, i):
        rolls[which, i].wait_recv()
        return roll_r[which, i, pl.ds(0, QUARTER), :].astype(F32)

    for which in range(4):
        for i in range(3):
            roll_s[which, i, pl.ds(32, 16), :] = jnp.zeros((16, D), BF16)
    roll_out(0, go_f, False)
    gather_turn()

    k_of = iota((TOK, 512), 0)
    lane = iota((TOK, 512), 1)
    side = (lane >= 256).astype(jnp.int32)
    j = lane - side * (256 + 72)
    s = over_six(jnp.maximum(j, 0))
    c = side * HALF + j - s * HALF
    inside = (j >= 0) & (j < 138)
    late = s > 11
    wanted = jnp.where(late, s - 11, s) * WIN + c
    hit = inside & (k_of == wanted)
    pick_a = jnp.where(hit & (s <= 11), 1.0, 0.0).astype(BF16)
    pick_b = jnp.where(hit & late, 1.0, 0.0).astype(BF16)
    high_a = dot((rel_ref[pl.ds(TOK - WIN, WIN), :] >> 4).astype(F32).astype(BF16), pick_a)
    low_a = dot((rel_ref[pl.ds(TOK - WIN, WIN), :] & 15).astype(F32).astype(BF16), pick_a)
    high_b = dot((rel_ref[pl.ds(0, WIN), :] >> 4).astype(F32).astype(BF16), pick_b)
    low_b = dot((rel_ref[pl.ds(0, WIN), :] & 15).astype(F32).astype(BF16), pick_b)
    idx_u[pl.ds(0, WIN), :] = ((high_a + high_b) * 16.0 + low_a + low_b).astype(jnp.int32)
    gather_turn()

    table = tab_ref[...]
    t_high = table.astype(BF16)
    rest = table - t_high.astype(F32)
    t_mid = rest.astype(BF16)
    t_low = (rest - t_mid.astype(F32)).astype(BF16)
    parts = jnp.concatenate([t_high, t_mid, t_low], axis=0)

    def choose(c1, _):
        chosen = idx_u[pl.ds(c1, 1), :]
        onehot = jnp.where(iota((TABLE, 512), 0) == chosen, 1.0, 0.0).astype(BF16)
        got3 = dot(parts, onehot)
        u_raw[c1] = got3[0:32] + got3[32:64] + got3[64:96]
        return 0

    lax.fori_loop(0, WIN, choose, 0)
    gather_turn()
    for th in range(2 * HEADS):
        rows = u_raw[:, th, :]
        u_ref[th, pl.ds(0, HALF), :] = rows[:HALF]
        u_ref[th, pl.ds(8, HALF), :] = rows[HALF:]

    def slide(th, _):
        left, right = u_ref[th, :, pl.ds(0, 256)], u_ref[th, :, pl.ds(256, 256)]
        first = iota((16, 256), 1) < 72
        for r in range(WIN):
            shift = (256 - HALF * (11 - r)) % 256
            a = pltpu.roll(left, shift, 1) if shift else left
            b = pltpu.roll(right, shift, 1) if shift else right
            value = jnp.where(first, a, b)[:, :TOK]
            bias[th, pl.ds(r * HALF, HALF), :] = value[:HALF]
            bias[th, pl.ds(72 + r * HALF, HALF), :] = value[8:8 + HALF]
        return 0

    lax.fori_loop(0, HEADS, slide, 0)
    gather_turn()

    n = iota((TOK, WIN), 0)
    right_half = (n >= 72).astype(jnp.int32)
    n = n - 72 * right_half
    row_of = over_six(n)
    col_of = right_half * HALF + n - row_of * HALF
    row_pick = jnp.where(iota((TOK, WIN), 1) == row_of, 1.0, 0.0).astype(BF16)
    per_row = dot(row_pick, cls_ref[...].astype(F32).astype(BF16))
    label = jnp.sum(
        jnp.where(iota((TOK, WIN), 1) == col_of, per_row, 0.0), axis=1, keepdims=True)
    member = jnp.where(iota((TOK, 128), 1) == label.astype(jnp.int32), 1.0, 0.0).astype(BF16)
    same[...] = dot_t(member, member)

    lax.fori_loop(HEADS, 2 * HEADS, slide, 0)

    even = jnp.where(iota((1, 128), 1) < 64, 1.0, 0.0).astype(BF16)
    masks = (even, (1.0 - even.astype(F32)).astype(BF16))

    def weight(u, block):
        return wbuf[u, block].reshape(D, BLOCK)

    def times_rows(left, u, block):
        result = None
        for c in range(4):
            term = dot_t(left(c), wbuf[u, c, block // 2, block % 2].reshape(BLOCK, BLOCK))
            result = term if result is None else result + term
        return result

    def project(which):
        for u in range(3):
            def step(i, _):
                first = pl.multiple_of(i * BLOCK, BLOCK)
                result = dot(norm_buf[...], weight(which * 4 + u, i))
                qkv[which, :, pl.ds(pl.multiple_of(u * D + first, BLOCK), BLOCK)] = result.astype(BF16)
                return 0
            lax.fori_loop(0, D // BLOCK, step, 0, unroll=4)

    def lanes(i, offset=0):
        return pl.ds(pl.multiple_of(offset + i * 128, 128), 128)

    def attend(which, first=0, last=HEADS // 2):
        def step(i, _):
            q2 = qkv[which, :, lanes(i)]
            k2 = qkv[which, :, lanes(i, D)]
            v2 = qkv[which, :, lanes(i, 2 * D)]
            mixed = None
            for e in range(2):
                score = dot_t(q2 * masks[e], k2) * 0.125 + bias[which * HEADS + 2 * i + e]
                if which:
                    score = jnp.where(same[...] > 0.5, score, LOW)
                power = jnp.exp(score - jnp.max(score, axis=1, keepdims=True))
                share_of = (power * (1.0 / jnp.sum(power, axis=1, keepdims=True))).astype(BF16)
                probs[which * HEADS + 2 * i + e] = share_of
                term = dot(share_of, v2 * masks[e])
                mixed = term if mixed is None else mixed + term
            att_stack[which, i // 2, pl.ds(0, TOK), lanes(i % 2)] = mixed.astype(BF16)
            return 0
        lax.fori_loop(first, last, step, 0, unroll=4)

    def attend_back(which, first=0, last=HEADS // 2):
        def step(i, _):
            q2 = qkv[which, :, lanes(i)]
            k2 = qkv[which, :, lanes(i, D)]
            v2 = qkv[which, :, lanes(i, 2 * D)]
            do2 = datt[:, lanes(i)]
            dq = dk = dv = None
            for e in range(2):
                share_of = probs[which * HEADS + 2 * i + e]
                up = do2 * masks[e]
                dp = dot_t(up, v2)
                share_f = share_of.astype(F32)
                mean = jnp.sum(dp * share_f, axis=1, keepdims=True)
                ds = (share_f * (dp - mean) * 0.125).astype(BF16)
                a = t_dot(share_of, up)
                b = dot(ds, k2 * masks[e])
                c = t_dot(ds, q2 * masks[e])
                dv = a if dv is None else dv + a
                dq = b if dq is None else dq + b
                dk = c if dk is None else dk + c
            dqkv[:, lanes(i)] = dq.astype(BF16)
            dqkv[:, lanes(i, D)] = dk.astype(BF16)
            dqkv[:, lanes(i, 2 * D)] = dv.astype(BF16)
            return 0
        lax.fori_loop(first, last, step, 0, unroll=4)

    def att_grad(source, which):
        for b in range(4):
            datt[:, pl.ds(b * BLOCK, BLOCK)] = times_rows(
                lambda c: source[pl.ds(0, TOK), pl.ds(c * BLOCK, BLOCK)],
                which * 4 + 3, b).astype(BF16)

    def normed_grad(which):
        for b in range(4):
            result = None
            for u in range(3):
                term = times_rows(
                    lambda c: dqkv[:, pl.ds(u * D + c * BLOCK, BLOCK)], which * 4 + u, b)
                result = term if result is None else result + term
            tmp_f[:, pl.ds(b * BLOCK, BLOCK)] = result.astype(BF16).astype(F32)

    sibs = {}

    def to_sibling(name, k, src, dst):
        c = copy(src, dst, sib_send.at[k], sib_recv.at[k], sibling)
        c.start()
        sibs[name] = c

    def send_att(m):
        for h in range(2):
            to_sibling((m, h), m * 3 + h, att_stack.at[m, h * 2 + other, pl.ds(0, TOK)],
                       att_stack.at[m, h * 2 + other, pl.ds(TOK, TOK)])

    def send_grad(m):
        to_sibling((m, 2), m * 3 + 2, g_stack.at[m, pl.ds(0, TOK)], g_stack.at[m, pl.ds(TOK, TOK)])

    def turn_att(m):
        for h in range(2):
            sibs[m, h].wait_recv()
            att_t[m, h] = att_stack[m, h * 2 + core].astype(F32).T.astype(BF16)

    steps = {}

    def ship(m, name, k, src, dst, device):
        c = copy(src, dst, red_send.at[m, k], red_recv.at[m, k], device)
        c.start()
        steps.setdefault((m, name), []).append(c)

    def landed(m, name):
        for c in steps[m, name]:
            c.wait_recv()

    def product(m, h, cols):
        return dot(att_t[m, h], g_stack[m, :, cols])

    def early_product():
        sibs[0, 2].wait_recv()
        for h in range(2):
            for c in range(4):
                cols = pl.ds(c * BLOCK, BLOCK)
                early[h, :, cols] = product(0, h, cols)

    def reduce_1(m):
        sibs[2 if m == 0 else 1, 2].wait_recv()
        for h in range(2):
            for c in range(4):
                cols = pl.ds(c * BLOCK, BLOCK)
                if m == 0:
                    value = product(2, h, cols) + early[h, :, cols]
                else:
                    value = product(1, h, cols)
                value = value.astype(BF16)
                if c < 2:
                    xs[m, h, :, :, :, cols] = value.reshape(NZ, 2, 16, BLOCK)
                else:
                    for q in range(2):
                        vs[m, (c - 2) * 2 + q, h] = value[:, q * 128:(q + 1) * 128].reshape(
                            NZ, 2, 16, 128)
        for d in (2, 1, 3):
            target = (x + d) % NX
            ship(m, "xx", d - 1, xs.at[m, target // 2, :, target % 2], xr.at[m, d - 1], at_x(d))
            ship(m, "vy", 2 + d, vs.at[m, (y + d) % NY], vr.at[m, d - 1], at_y(d))

    def reduce_2(m):
        landed(m, "xx")
        value = xs[m, xh, :, xl].astype(F32)
        for d in range(NX - 1):
            value = value + xr[m, d].astype(F32)
        zs[m] = value.astype(BF16)
        for d in (4, 3, 5, 2, 6, 1, 7):
            ship(m, "xz", 5 + d, zs.at[m, (z + d) % NZ], zr.at[m, d - 1], at_z(d))
        landed(m, "vy")
        value = vs[m, y].astype(F32)
        for d in range(NY - 1):
            value = value + vr[m, d].astype(F32)
        ws[m] = value.astype(BF16)
        for d in (2, 1, 3):
            target = (x + d) % NX
            ship(m, "vx", 12 + d, ws.at[m, target // 2, :, target % 2], wr.at[m, d - 1], at_x(d))

    def reduce_3(m):
        landed(m, "vx")
        value = ws[m, xh, :, xl].astype(F32)
        for d in range(NX - 1):
            value = value + wr[m, d].astype(F32)
        us[m] = value.astype(BF16)
        for d in (4, 3, 5, 2, 6, 1, 7):
            ship(m, "vz", 15 + d, us.at[m, (z + d) % NZ], ur.at[m, d - 1], at_z(d))
        landed(m, "xz")
        value = zs[m, z].astype(F32)
        for d in range(NZ - 1):
            value = value + zr[m, d].astype(F32)
        ys[m, y] = value.astype(BF16)
        for d in range(1, NY):
            ship(m, "xy", 22 + d, ys.at[m, y], ys.at[m, y], at_y(d))

    def reduce_4(m):
        landed(m, "vz")
        value = us[m, z].astype(F32)
        for d in range(NZ - 1):
            value = value + ur[m, d].astype(F32)
        os[m, y] = value.astype(BF16)
        for d in range(1, NY):
            ship(m, "vo", 25 + d, os.at[m, y], os.at[m, y], at_y(d))

    def reduce_end(m, target):
        landed(m, "xy")
        value = ys[m, 0].astype(F32)
        for i in range(1, NY):
            value = value + ys[m, i].astype(F32)
        target[:, pl.ds(0, 512)] = value
        landed(m, "vo")
        for i in range(NY):
            target[:, pl.ds(512 + i * 128, 128)] = os[m, i].astype(F32)

    unit, _ = norm_parts(tok_f[...])
    norm_buf[...] = (unit * gain1_ref[...]).astype(BF16)
    g_stack[0, pl.ds(0, TOK), :] = go_f[...].astype(BF16)
    send_grad(0)
    sh_f[pl.ds(0, QUARTER), :] = go_f[pl.ds(3 * QUARTER, QUARTER), :]
    for i in range(3):
        sh_f[pl.ds((i + 1) * QUARTER, QUARTER), :] = roll_in(0, i)
    g_stack[1, pl.ds(0, TOK), :] = sh_f[...].astype(BF16)
    send_grad(1)
    gather_until((0, 1, 2))
    project(0)
    gather_turn()
    attend(0)
    send_att(0)
    gather_until((3,))
    for b in range(4):
        cols = pl.ds(b * BLOCK, BLOCK)
        result = tok_f[:, cols]
        for h in range(4):
            result = result + dot(att_stack[0, h, pl.ds(0, TOK), :],
                                  wbuf[3, b, h // 2, h % 2].reshape(BLOCK, BLOCK))
        mid_f[:, cols] = result.astype(BF16).astype(F32)
    roll_out(1, mid_f, False)
    for h in range(4):
        tmp_f[:, pl.ds(h * BLOCK, BLOCK)] = att_stack[0, h, pl.ds(0, TOK), :].astype(F32)
    roll_out(3, tmp_f, False)
    turn_att(0)
    early_product()
    sh_f[pl.ds(0, QUARTER), :] = mid_f[pl.ds(3 * QUARTER, QUARTER), :]
    for i in range(3):
        sh_f[pl.ds((i + 1) * QUARTER, QUARTER), :] = roll_in(1, i)
    unit, _ = norm_parts(sh_f[...])
    norm_buf[...] = (unit * gain2_ref[...]).astype(BF16)
    mid_f[pl.ds(0, QUARTER), :] = tmp_f[pl.ds(3 * QUARTER, QUARTER), :]
    for i in range(3):
        mid_f[pl.ds((i + 1) * QUARTER, QUARTER), :] = roll_in(3, i)
    for h in range(4):
        att_stack[2, h, pl.ds(0, TOK), :] = mid_f[:, pl.ds(h * BLOCK, BLOCK)].astype(BF16)
    send_att(2)
    gather_until(range(8))
    att_grad(g_stack.at[1], 1)
    project(1)
    attend(1)
    send_att(1)
    turn_att(2)
    attend_back(1)
    turn_att(1)
    reduce_1(1)
    normed_grad(1)
    mid_f[...] = norm_back(sh_f[...], gain2_ref[...], tmp_f[...])
    g_stack[2, pl.ds(0, TOK), :] = mid_f[...].astype(BF16)
    send_grad(2)
    roll_out(2, mid_f, True)
    reduce_1(0)
    sh_f[pl.ds(3 * QUARTER, QUARTER), :] = mid_f[pl.ds(0, QUARTER), :].astype(BF16).astype(F32)
    for i, quarter in enumerate((2, 1, 0)):
        sh_f[pl.ds(quarter * QUARTER, QUARTER), :] = roll_in(2, i)
    mid_f[...] = (go_f[...] + sh_f[...]).astype(BF16).astype(F32)
    norm_buf[...] = mid_f[...].astype(BF16)
    att_grad(norm_buf, 0)
    reduce_2(1)
    attend_back(0, 0, 4)
    reduce_2(0)
    attend_back(0, 4, 8)
    reduce_3(1)
    normed_grad(0)
    reduce_3(0)
    sh_f[...] = mid_f[...] + norm_back(tok_f[...], gain1_ref[...], tmp_f[...]).astype(BF16).astype(F32)
    for r in range(WIN):
        rows = jnp.concatenate(
            [sh_f[pl.ds(r * HALF, HALF), :], sh_f[pl.ds(72 + r * HALF, HALF), :]], axis=0)
        out_ref[0, r] = rows.astype(BF16)
    reduce_4(1)
    reduce_4(0)
    reduce_end(1, og2_ref)
    reduce_end(0, og1_ref)
    for group_of in (flights, rolls, sibs):
        for c in group_of.values():
            c.wait_send()
    for some in steps.values():
        for c in some:
            c.wait_send()


def on_device(
    tokens, grad_out, first_gain, first_qkv_weight, first_out_weight, first_bias,
    second_gain, second_qkv_weight, second_out_weight, second_bias, rel_index, classes,
):
    table = jnp.concatenate([first_bias, second_bias], axis=1).T
    table = jnp.pad(table, ((0, 0), (0, TABLE - table.shape[1])))
    vmem = pl.BlockSpec(memory_space=pltpu.VMEM)
    hbm = pl.BlockSpec(memory_space=pl.ANY)
    dma = pltpu.SemaphoreType.DMA
    return pl.pallas_call(
        kernel,
        out_shape=(
            jax.ShapeDtypeStruct((1, WIN, WIN, D), BF16),
            jax.ShapeDtypeStruct((16, D), F32),
            jax.ShapeDtypeStruct((16, D), F32),
        ),
        in_specs=[vmem] * 4 + [hbm] * 4 + [vmem] * 3,
        out_specs=(vmem, vmem, vmem),
        scratch_shapes=[
            pltpu.VMEM((8, NY, 2, 2, NZ, 2, 16, BLOCK), BF16),
            pltpu.VMEM((2 * HEADS, TOK, TOK), F32),
            pltpu.VMEM((16, 512), jnp.int32),
            pltpu.VMEM((WIN, 2 * HEADS, 512), F32),
            pltpu.VMEM((2 * HEADS, 16, 512), F32),
            pltpu.VMEM((TOK, TOK), F32),
            pltpu.VMEM((2 * HEADS, TOK, TOK), BF16),
            pltpu.VMEM((2, TOK, 3 * D), BF16),
            pltpu.VMEM((TOK, 3 * D), BF16),
            pltpu.VMEM((TOK, D), BF16),
            pltpu.VMEM((TOK, D), BF16),
            pltpu.VMEM((TOK, D), F32),
            pltpu.VMEM((TOK, D), F32),
            pltpu.VMEM((TOK, D), F32),
            pltpu.VMEM((TOK, D), F32),
            pltpu.VMEM((TOK, D), F32),
            pltpu.VMEM((3, 2 * TOK, D), BF16),
            pltpu.VMEM((3, 4, 2 * TOK, BLOCK), BF16),
            pltpu.VMEM((4, 3, 48, D), BF16),
            pltpu.VMEM((4, 3, 48, D), BF16),
            pltpu.VMEM((3, 2, BLOCK, 2 * TOK), BF16),
            pltpu.VMEM((2, BLOCK, D), F32),
            pltpu.VMEM((2, 2, NZ, 2, 16, 512), BF16),
            pltpu.VMEM((2, NX - 1, NZ, 16, 512), BF16),
            pltpu.VMEM((2, NZ, 16, 512), BF16),
            pltpu.VMEM((2, NZ - 1, 16, 512), BF16),
            pltpu.VMEM((2, NY, 16, 512), BF16),
            pltpu.VMEM((2, NY, 2, NZ, 2, 16, 128), BF16),
            pltpu.VMEM((2, NY - 1, 2, NZ, 2, 16, 128), BF16),
            pltpu.VMEM((2, 2, NZ, 2, 16, 128), BF16),
            pltpu.VMEM((2, NX - 1, NZ, 16, 128), BF16),
            pltpu.VMEM((2, NZ, 16, 128), BF16),
            pltpu.VMEM((2, NZ - 1, 16, 128), BF16),
            pltpu.VMEM((2, NY, 16, 128), BF16),
            dma((8,)),
            dma((8, 24)), dma((8, 24)),
            dma((4, 3)), dma((4, 3)),
            dma((9,)), dma((9,)),
            dma((2, 29)), dma((2, 29)),
        ],
        compiler_params=pltpu.CompilerParams(
            collective_id=0, has_side_effects=True, vmem_limit_bytes=56 * 1024 * 1024
        ),
        name="window_blocks",
    )(
        tokens, grad_out, first_gain[None], second_gain[None],
        first_qkv_weight, first_out_weight, second_qkv_weight, second_out_weight,
        table, rel_index, classes,
    )


def solution(mesh):
    tile = P("rep", "lat", "lon", None)
    rows = P(("lat", "lon"), None)
    in_specs = (tile, tile, P(), rows, rows, P(), P(), rows, rows, P(), P(), P("lat", "lon"))
    return jax.shard_map(
        on_device, mesh=mesh, in_specs=in_specs, out_specs=(tile, rows, rows), check_vma=False
    )
```

```python
import jax
import jax.numpy as jnp
from jax import lax
from jax.experimental import pallas as pl
from jax.experimental.pallas import tpu as pltpu
from jax.sharding import PartitionSpec as P

HEADS = 16
WIN = 12
HALF = WIN // 2
TOK = WIN * WIN
QUARTER = HALF * HALF
D = 1024
EPSILON = 1e-05
NX, NY, NZ = 4, 4, 8
TABLE = 640
BLOCK = 256
LOW = -1e30
MESH = pl.DeviceIdType.MESH
F32 = jnp.float32
BF16 = jnp.bfloat16

ORDERS = ("zxy", "zyx", "xyz", "zxy", "zyx", "zxy", "xyz", "zyx")
STAGES = 7


def dot(a, b):
    return jnp.dot(a, b, preferred_element_type=F32)


def dot_t(a, b):
    return lax.dot_general(a, b, (((1,), (1,)), ((), ())), preferred_element_type=F32)


def t_dot(a, b):
    return lax.dot_general(a, b, (((0,), (0,)), ((), ())), preferred_element_type=F32)


def iota(shape, dim):
    return lax.broadcasted_iota(jnp.int32, shape, dim)


def over_six(n):
    return (n * 10923) >> 16


def qkv_column(n):
    return (n % 3) * D + (n // 3) * BLOCK


def norm_parts(x):
    centered = x - jnp.mean(x, axis=-1, keepdims=True)
    scale = lax.rsqrt(jnp.mean(centered * centered, axis=-1, keepdims=True) + EPSILON)
    return centered * scale, scale


def norm_back(x, gain, grad):
    unit, scale = norm_parts(x)
    g = grad * gain
    return scale * (
        g - jnp.mean(g, axis=-1, keepdims=True) - unit * jnp.mean(g * unit, axis=-1, keepdims=True)
    )


def kernel(
    tokens_ref, grad_ref, gain1_ref, gain2_ref, wq1_ref, wo1_ref, wq2_ref, wo2_ref,
    bias1_ref, bias2_ref, rel_in, cls_in,
    out_ref, og1_ref, og2_ref,
    tokens_v, grad_v, bias1_v, bias2_v, rel_ref, cls_ref, tab,
    wbuf, bias, idx_u, u_raw, u_ref, same, probs, qkv, dqkv, norm_buf, datt,
    tok_f, go_f, mid_f, sh_f, tmp_f, g_stack, att_stack, roll_s, roll_r,
    partial, att_t, early, xs, xr, zs, zr, ys, vs, vr, ws, wr, us, ur, os,
    load_sem, w_local, w_send, w_recv, roll_send, roll_recv, sib_send, sib_recv, red_send, red_recv,
):
    lat, lon, y = lax.axis_index("lat"), lax.axis_index("lon"), lax.axis_index("rep")
    xh, core = lat // 2, lat % 2
    z, xl = lon // 2, lon % 2
    x = xh * 2 + xl
    other = 1 - core

    def at_x(d):
        n = (x + d) % NX
        return ((n // 2) * 2 + core, z * 2 + n % 2, y)

    def at_z(d):
        return (lat, ((z + d) % NZ) * 2 + xl, y)

    def at_y(d):
        return (lat, lon, (y + d) % NY)

    sibling = (xh * 2 + other, lon, y)

    def at_roll(a, b):
        return ((lat + a + 4) % 4, (lon + b + 16) % 16, y)

    def copy(src, dst, send, recv, device):
        return pltpu.make_async_remote_copy(
            src_ref=src, dst_ref=dst, send_sem=send, recv_sem=recv,
            device_id=device, device_id_type=MESH,
        )

    barrier = pltpu.get_barrier_semaphore()
    partners = [at_z(d) for d in range(1, NZ)] + [at_x(d) for d in range(1, NX)]
    partners += [at_y(d) for d in range(1, NY)] + [sibling]
    partners += [at_roll(*s) for s in ((1, 0), (-1, 0), (0, 1), (0, -1), (1, 1), (-1, -1))]
    for partner in partners:
        pl.semaphore_signal(barrier, inc=1, device_id=partner, device_id_type=MESH)
    local = []
    for u in range(8):
        source = (wq1_ref, wo1_ref, wq2_ref, wo2_ref)[(u // 4) * 2 + (u % 4) // 3]
        n = (u % 4) * 4 + y
        column = qkv_column(n) if u % 4 < 3 else y * BLOCK
        local.append(
            pltpu.make_async_copy(
                source.at[:, pl.ds(pl.multiple_of(column, BLOCK), BLOCK)],
                wbuf.at[u, y, xh, core, z, xl], w_local.at[u],
            )
        )
        local[-1].start()

    loads = [
        pltpu.make_async_copy(source, target, load_sem.at[i])
        for i, (source, target) in enumerate((
            (grad_ref, grad_v), (rel_in, rel_ref), (tokens_ref, tokens_v),
            (bias1_ref, bias1_v), (bias2_ref, bias2_v), (cls_in, cls_ref)))
    ]
    for c in loads:
        c.start()

    pl.semaphore_wait(barrier, len(partners))
    for c in local:
        c.wait()

    flights, counts = {}, [0] * 8

    def send(u, tag, src, device):
        k = counts[u]
        counts[u] += 1
        c = copy(src, src, w_send.at[u, k], w_recv.at[u, k], device)
        c.start()
        flights[u, k] = c
        waits.setdefault((u, tag), []).append(c)

    waits = {}

    def got(u, tag):
        for c in waits[u, tag]:
            c.wait_recv()

    def element(u):
        return wbuf.at[u, y, xh, core, z, xl]

    def wrap(n, size):
        return (n + size) % size

    def spread(u, tag, src, at, size):
        for d in sorted(range(1, size), key=lambda d: -min(d, size - d)):
            send(u, tag, src, at(d))

    def share(u, src):
        send(u, "share", src, sibling)

    def stage_zxy(u, stage):
        def plane(d):
            return wbuf.at[u, wrap(y + d, NY), :, core]

        def half(d, h):
            return wbuf.at[u, wrap(y + d, NY), h, core]

        if stage == 0:
            spread(u, 0, element(u), at_z, NZ)
        if stage == 1:
            got(u, 0)
            spread(u, 1, wbuf.at[u, y, xh, core, :, xl], at_x, NX)
        if stage == 2:
            got(u, 1)
            send(u, "r1", half(0, 0), at_y(1))
            send(u, "l1", half(0, 1), at_y(3))
            send(u, "r2", half(0, 1), at_y(1))
            send(u, "l2", half(0, 0), at_y(3))
            share(u, plane(0))
        if stage == 3:
            got(u, "r1")
            send(u, "far", half(-1, 0), at_y(1))
            got(u, "l1")
            send(u, "far", half(1, 1), at_y(3))
        if stage == 4:
            got(u, "r2")
            share(u, plane(-1))
            got(u, "l2")
            share(u, plane(1))
        if stage == 5:
            got(u, "far")
            share(u, plane(2))

    def stage_zyx(u, stage):
        def column(d):
            n = wrap(x + d, NX)
            return wbuf.at[u, :, n // 2, core, :, n % 2]

        def half(d, h):
            n = wrap(x + d, NX)
            return wbuf.at[u, pl.ds(2 * h, 2), n // 2, core, :, n % 2]

        if stage == 0:
            spread(u, 0, element(u), at_z, NZ)
        if stage == 1:
            got(u, 0)
            spread(u, 1, wbuf.at[u, y, xh, core, :, xl], at_y, NY)
        if stage == 2:
            got(u, 1)
            send(u, "r1", half(0, 0), at_x(1))
            send(u, "l1", half(0, 1), at_x(3))
            send(u, "r2", half(0, 1), at_x(1))
            send(u, "l2", half(0, 0), at_x(3))
            share(u, column(0))
        if stage == 3:
            got(u, "r1")
            send(u, "far", half(-1, 0), at_x(1))
            got(u, "l1")
            send(u, "far", half(1, 1), at_x(3))
        if stage == 4:
            got(u, "r2")
            share(u, column(-1))
            got(u, "l2")
            share(u, column(1))
        if stage == 5:
            got(u, "far")
            share(u, column(2))

    def stage_xyz(u, stage):
        def group(d):
            return wbuf.at[u, :, :, core, wrap(z + d, NZ)]

        def half(d, h):
            return wbuf.at[u, pl.ds(2 * h, 2), :, core, wrap(z + d, NZ)]

        if stage == 0:
            spread(u, 0, element(u), at_x, NX)
        if stage == 1:
            got(u, 0)
            spread(u, 1, wbuf.at[u, y, :, core, z], at_y, NY)
        if stage == 2:
            got(u, 1)
            send(u, "r2", group(0), at_z(2))
            send(u, "l2", group(0), at_z(6))
            send(u, "r1", group(0), at_z(1))
            send(u, "l1", group(0), at_z(7))
            share(u, group(0))
        if stage == 3:
            got(u, "r2")
            send(u, "far", half(-2, 0), at_z(2))
            send(u, "far", group(-2), at_z(1))
            got(u, "l2")
            send(u, "far", half(2, 1), at_z(6))
            send(u, "far", group(2), at_z(7))
        if stage == 4:
            got(u, "r1")
            got(u, "l1")
            for d in (-2, -1, 1, 2):
                share(u, group(d))
        if stage == 5:
            got(u, "far")
            for d in (-3, 3, 4):
                share(u, group(d))

    def gather_stage(u, stage):
        if 0 <= stage < STAGES:
            {"zxy": stage_zxy, "zyx": stage_zyx, "xyz": stage_xyz}[ORDERS[u]](u, stage)
        if stage == 6:
            got(u, "share")

    def gather(stage, *units):
        for u in units:
            gather_stage(u, stage)

    gather(0, 0, 1, 2, 3, 4, 5, 6, 7)
    for c in loads:
        c.wait()

    for r in range(WIN):
        for source, target in ((tokens_v, tok_f), (grad_v, go_f)):
            rows = source[0, r].astype(F32)
            target[pl.ds(r * HALF, HALF), :] = rows[:HALF]
            target[pl.ds(72 + r * HALF, HALF), :] = rows[HALF:]

    rolls = {}

    def roll_out(which, source, back):
        to = 1 if back else -1
        places = ((1, (to, 0)), (2, (0, to)), (3, (to, to))) if back else (
            (2, (to, 0)), (1, (0, to)), (0, (to, to)))
        for i, (quarter, shift) in enumerate(places):
            rows = source[pl.ds(quarter * QUARTER, QUARTER), :]
            roll_s[which, i] = jnp.concatenate(
                [rows[:, c * BLOCK:(c + 1) * BLOCK] for c in range(4)], axis=0).astype(BF16)
            c = copy(roll_s.at[which, i], roll_r.at[which, i],
                     roll_send.at[which, i], roll_recv.at[which, i], at_roll(*shift))
            c.start()
            rolls[which, i] = c

    def roll_in(which, i):
        rolls[which, i].wait_recv()
        rows = roll_r[which, i].astype(F32)
        return jnp.concatenate(
            [rows[c * QUARTER:(c + 1) * QUARTER] for c in range(4)], axis=1)

    roll_out(0, go_f, False)

    k_of = iota((TOK, 512), 0)
    lane = iota((TOK, 512), 1)
    side = (lane >= 256).astype(jnp.int32)
    j = lane - side * (256 + 72)
    s = over_six(jnp.maximum(j, 0))
    c = side * HALF + j - s * HALF
    inside = (j >= 0) & (j < 138)
    late = s > 11
    wanted = jnp.where(late, s - 11, s) * WIN + c
    hit = inside & (k_of == wanted)
    pick_a = jnp.where(hit & (s <= 11), 1.0, 0.0).astype(BF16)
    pick_b = jnp.where(hit & late, 1.0, 0.0).astype(BF16)
    high_a = dot((rel_ref[pl.ds(TOK - WIN, WIN), :] >> 4).astype(F32).astype(BF16), pick_a)
    low_a = dot((rel_ref[pl.ds(TOK - WIN, WIN), :] & 15).astype(F32).astype(BF16), pick_a)
    high_b = dot((rel_ref[pl.ds(0, WIN), :] >> 4).astype(F32).astype(BF16), pick_b)
    low_b = dot((rel_ref[pl.ds(0, WIN), :] & 15).astype(F32).astype(BF16), pick_b)
    idx_u[pl.ds(0, WIN), :] = ((high_a + high_b) * 16.0 + low_a + low_b).astype(jnp.int32)
    gather(1, 0, 1, 2)

    tab[...] = jnp.zeros_like(tab)
    entries = bias1_v.shape[1]
    tab[pl.ds(0, HEADS), pl.ds(0, entries)] = bias1_v[...]
    tab[pl.ds(HEADS, HEADS), pl.ds(0, entries)] = bias2_v[...]
    table = tab[...]
    t_high = table.astype(BF16)
    rest = table - t_high.astype(F32)
    t_mid = rest.astype(BF16)
    t_low = (rest - t_mid.astype(F32)).astype(BF16)
    parts = jnp.concatenate([t_high, t_mid, t_low], axis=0)

    def choose(c1, _):
        chosen = idx_u[pl.ds(c1, 1), :]
        onehot = jnp.where(iota((TABLE, 512), 0) == chosen, 1.0, 0.0).astype(BF16)
        got3 = dot(parts, onehot)
        u_raw[c1] = got3[0:32] + got3[32:64] + got3[64:96]
        return 0

    lax.fori_loop(0, WIN, choose, 0)
    gather(2, 0, 1, 2)
    gather(1, 3, 4, 6, 5, 7)
    for th in range(2 * HEADS):
        rows = u_raw[:, th, :]
        u_ref[th, pl.ds(0, HALF), :] = rows[:HALF]
        u_ref[th, pl.ds(8, HALF), :] = rows[HALF:]

    def slide(th, _):
        left, right = u_ref[th, :, pl.ds(0, 256)], u_ref[th, :, pl.ds(256, 256)]
        first = iota((16, 256), 1) < 72
        for r in range(WIN):
            shift = (256 - HALF * (11 - r)) % 256
            a = pltpu.roll(left, shift, 1) if shift else left
            b = pltpu.roll(right, shift, 1) if shift else right
            value = jnp.where(first, a, b)[:, :TOK]
            bias[th, pl.ds(r * HALF, HALF), :] = value[:HALF]
            bias[th, pl.ds(72 + r * HALF, HALF), :] = value[8:8 + HALF]
        return 0

    lax.fori_loop(0, HEADS, slide, 0)

    n = iota((TOK, WIN), 0)
    right_half = (n >= 72).astype(jnp.int32)
    n = n - 72 * right_half
    row_of = over_six(n)
    col_of = right_half * HALF + n - row_of * HALF
    row_pick = jnp.where(iota((TOK, WIN), 1) == row_of, 1.0, 0.0).astype(BF16)
    per_row = dot(row_pick, cls_ref[...].astype(F32).astype(BF16))
    label = jnp.sum(
        jnp.where(iota((TOK, WIN), 1) == col_of, per_row, 0.0), axis=1, keepdims=True)
    member = jnp.where(iota((TOK, 128), 1) == label.astype(jnp.int32), 1.0, 0.0).astype(BF16)
    same[...] = dot_t(member, member)

    gather(3, 0, 1)
    gather(2, 3, 4)
    lax.fori_loop(HEADS, 2 * HEADS, slide, 0)

    even = jnp.where(iota((1, 128), 1) < 64, 1.0, 0.0).astype(BF16)
    masks = (even, (1.0 - even.astype(F32)).astype(BF16))

    def weight(u, block):
        return wbuf[u, block].reshape(D, BLOCK)

    def times_rows(left, u, block):
        result = None
        for c in range(4):
            term = dot_t(left(c), wbuf[u, c, block // 2, block % 2].reshape(BLOCK, BLOCK))
            result = term if result is None else result + term
        return result

    def project(which, own, *parts_of):
        half = core if own else other
        for u in parts_of:
            for i in range(4):
                cols = pl.ds(i * BLOCK, BLOCK)
                result = None if own else partial[u, :, cols]
                for h in range(2):
                    rows = pl.ds(pl.multiple_of(h * 512 + half * BLOCK, BLOCK), BLOCK)
                    term = dot(norm_buf[:, rows], wbuf[which * 4 + u, i, h, half].reshape(BLOCK, BLOCK))
                    result = term if result is None else result + term
                if own:
                    partial[u, :, cols] = result
                else:
                    qkv[which, :, pl.ds(qkv_column(u * 4 + i), BLOCK)] = result.astype(BF16)

    def lanes(i, offset=0):
        return pl.ds(pl.multiple_of(offset + i * 128, 128), 128)

    def attend(which, first=0, last=HEADS // 2):
        def step(i, _):
            q2 = qkv[which, :, lanes(i)]
            k2 = qkv[which, :, lanes(i, D)]
            v2 = qkv[which, :, lanes(i, 2 * D)]
            mixed = None
            for e in range(2):
                score = dot_t(q2 * masks[e], k2) * 0.125 + bias[which * HEADS + 2 * i + e]
                if which:
                    score = jnp.where(same[...] > 0.5, score, LOW)
                power = jnp.exp(score - jnp.max(score, axis=1, keepdims=True))
                share_of = (power * (1.0 / jnp.sum(power, axis=1, keepdims=True))).astype(BF16)
                probs[which * HEADS + 2 * i + e] = share_of
                term = dot(share_of, v2 * masks[e])
                mixed = term if mixed is None else mixed + term
            att_stack[which, i // 2, pl.ds(0, TOK), lanes(i % 2)] = mixed.astype(BF16)
            return 0
        lax.fori_loop(first, last, step, 0, unroll=4)

    def attend_back(which, first=0, last=HEADS // 2):
        def step(i, _):
            q2 = qkv[which, :, lanes(i)]
            k2 = qkv[which, :, lanes(i, D)]
            v2 = qkv[which, :, lanes(i, 2 * D)]
            do2 = datt[:, lanes(i)]
            dq = dk = dv = None
            for e in range(2):
                share_of = probs[which * HEADS + 2 * i + e]
                up = do2 * masks[e]
                dp = dot_t(up, v2)
                share_f = share_of.astype(F32)
                mean = jnp.sum(dp * share_f, axis=1, keepdims=True)
                ds = (share_f * (dp - mean) * 0.125).astype(BF16)
                a = t_dot(share_of, up)
                b = dot(ds, k2 * masks[e])
                c = t_dot(ds, q2 * masks[e])
                dv = a if dv is None else dv + a
                dq = b if dq is None else dq + b
                dk = c if dk is None else dk + c
            dqkv[:, lanes(i)] = dq.astype(BF16)
            dqkv[:, lanes(i, D)] = dk.astype(BF16)
            dqkv[:, lanes(i, 2 * D)] = dv.astype(BF16)
            return 0
        lax.fori_loop(first, last, step, 0, unroll=4)

    def att_grad(source, which):
        for b in range(4):
            datt[:, pl.ds(b * BLOCK, BLOCK)] = times_rows(
                lambda c: source[pl.ds(0, TOK), pl.ds(c * BLOCK, BLOCK)],
                which * 4 + 3, b).astype(BF16)

    def normed_grad(which):
        for b in range(4):
            result = None
            for u in range(3):
                term = times_rows(
                    lambda c: dqkv[:, pl.ds(qkv_column(u * 4 + c), BLOCK)], which * 4 + u, b)
                result = term if result is None else result + term
            tmp_f[:, pl.ds(b * BLOCK, BLOCK)] = result.astype(BF16).astype(F32)

    sibs = {}

    def to_sibling(name, k, src, dst):
        c = copy(src, dst, sib_send.at[k], sib_recv.at[k], sibling)
        c.start()
        sibs[name] = c

    def send_att(m):
        for h in range(2):
            to_sibling((m, h), m * 3 + h, att_stack.at[m, h * 2 + other, pl.ds(0, TOK)],
                       att_stack.at[m, h * 2 + other, pl.ds(TOK, TOK)])

    def send_grad(m):
        to_sibling((m, 2), m * 3 + 2, g_stack.at[m, pl.ds(0, TOK)], g_stack.at[m, pl.ds(TOK, TOK)])

    def turn_att(m):
        for h in range(2):
            sibs[m, h].wait_recv()
            att_t[m, h] = att_stack[m, h * 2 + core].astype(F32).T.astype(BF16)

    steps = {}

    def ship(m, name, k, src, dst, device):
        c = copy(src, dst, red_send.at[m, k], red_recv.at[m, k], device)
        c.start()
        steps.setdefault((m, name), []).append(c)

    def landed(m, name):
        for c in steps[m, name]:
            c.wait_recv()

    def product(m, h, cols):
        return dot(att_t[m, h], g_stack[m, :, cols])

    def early_product():
        sibs[0, 2].wait_recv()
        for h in range(2):
            for c in range(4):
                cols = pl.ds(c * BLOCK, BLOCK)
                early[h, :, cols] = product(0, h, cols)

    def reduce_1(m):
        sibs[2 if m == 0 else 1, 2].wait_recv()
        for h in range(2):
            for c in range(4):
                cols = pl.ds(c * BLOCK, BLOCK)
                if m == 0:
                    value = product(2, h, cols) + early[h, :, cols]
                else:
                    value = product(1, h, cols)
                value = value.astype(BF16)
                if c < 2:
                    xs[m, h, :, :, :, cols] = value.reshape(NZ, 2, 16, BLOCK)
                else:
                    for q in range(2):
                        vs[m, (c - 2) * 2 + q, h] = value[:, q * 128:(q + 1) * 128].reshape(
                            NZ, 2, 16, 128)
        for d in (2, 1, 3):
            target = (x + d) % NX
            ship(m, "xx", d - 1, xs.at[m, target // 2, :, target % 2], xr.at[m, d - 1], at_x(d))
            ship(m, "vy", 2 + d, vs.at[m, (y + d) % NY], vr.at[m, d - 1], at_y(d))

    def reduce_2(m):
        landed(m, "xx")
        value = xs[m, xh, :, xl].astype(F32)
        for d in range(NX - 1):
            value = value + xr[m, d].astype(F32)
        zs[m] = value.astype(BF16)
        for d in (4, 3, 5, 2, 6, 1, 7):
            ship(m, "xz", 5 + d, zs.at[m, (z + d) % NZ], zr.at[m, d - 1], at_z(d))
        landed(m, "vy")
        value = vs[m, y].astype(F32)
        for d in range(NY - 1):
            value = value + vr[m, d].astype(F32)
        ws[m] = value.astype(BF16)
        for d in (2, 1, 3):
            target = (x + d) % NX
            ship(m, "vx", 12 + d, ws.at[m, target // 2, :, target % 2], wr.at[m, d - 1], at_x(d))

    def reduce_3(m):
        landed(m, "vx")
        value = ws[m, xh, :, xl].astype(F32)
        for d in range(NX - 1):
            value = value + wr[m, d].astype(F32)
        us[m] = value.astype(BF16)
        for d in (4, 3, 5, 2, 6, 1, 7):
            ship(m, "vz", 15 + d, us.at[m, (z + d) % NZ], ur.at[m, d - 1], at_z(d))
        landed(m, "xz")
        value = zs[m, z].astype(F32)
        for d in range(NZ - 1):
            value = value + zr[m, d].astype(F32)
        ys[m, y] = value.astype(BF16)
        for d in range(1, NY):
            ship(m, "xy", 22 + d, ys.at[m, y], ys.at[m, y], at_y(d))

    def reduce_4(m):
        landed(m, "vz")
        value = us[m, z].astype(F32)
        for d in range(NZ - 1):
            value = value + ur[m, d].astype(F32)
        os[m, y] = value.astype(BF16)
        for d in range(1, NY):
            ship(m, "vo", 25 + d, os.at[m, y], os.at[m, y], at_y(d))

    def reduce_end(m, target):
        landed(m, "xy")
        value = ys[m, 0].astype(F32)
        for i in range(1, NY):
            value = value + ys[m, i].astype(F32)
        target[:, pl.ds(0, 512)] = value
        landed(m, "vo")
        for i in range(NY):
            target[:, pl.ds(512 + i * 128, 128)] = os[m, i].astype(F32)

    gather(3, 2)
    gather(2, 6)
    gather(4, 0, 1)
    unit, _ = norm_parts(tok_f[...])
    norm_buf[...] = (unit * gain1_ref[...]).astype(BF16)
    g_stack[0, pl.ds(0, TOK), :] = go_f[...].astype(BF16)
    send_grad(0)
    sh_f[pl.ds(0, QUARTER), :] = go_f[pl.ds(3 * QUARTER, QUARTER), :]
    for i in range(3):
        sh_f[pl.ds((i + 1) * QUARTER, QUARTER), :] = roll_in(0, i)
    g_stack[1, pl.ds(0, TOK), :] = sh_f[...].astype(BF16)
    send_grad(1)
    gather(5, 0, 1)
    gather(4, 2)
    project(0, True, 0, 1)
    gather(3, 3, 4)
    gather(2, 5, 7)
    gather(6, 0, 1)
    project(0, False, 0, 1)
    gather(5, 2)
    attend(0, 0, 4)
    gather(4, 3, 4)
    project(0, True, 2)
    gather(6, 2)
    project(0, False, 2)
    gather(5, 3, 4)
    attend(0, 4, 8)
    send_att(0)
    gather(3, 5, 7)
    gather(3, 6)
    gather(6, 3)
    for b in range(4):
        cols = pl.ds(b * BLOCK, BLOCK)
        result = tok_f[:, cols]
        for h in range(4):
            result = result + dot(att_stack[0, h, pl.ds(0, TOK), :],
                                  wbuf[3, b, h // 2, h % 2].reshape(BLOCK, BLOCK))
        mid_f[:, cols] = result.astype(BF16).astype(F32)
    roll_out(1, mid_f, False)
    turn_att(0)
    gather(4, 5, 7)
    gather(4, 6)
    early_product()
    gather(6, 4)
    gather(5, 5, 7)
    sh_f[pl.ds(0, QUARTER), :] = mid_f[pl.ds(3 * QUARTER, QUARTER), :]
    for i in range(3):
        sh_f[pl.ds((i + 1) * QUARTER, QUARTER), :] = roll_in(1, i)
    unit, _ = norm_parts(sh_f[...])
    norm_buf[...] = (unit * gain2_ref[...]).astype(BF16)
    project(1, True, 0)
    project(1, False, 0)
    project(1, True, 1)
    gather(6, 5)
    project(1, False, 1)
    gather(5, 6)
    project(1, True, 2)
    attend(1, 0, 4)
    gather(6, 6)
    project(1, False, 2)
    attend(1, 4, 8)
    send_att(1)
    for h in range(4):
        tmp_f[:, pl.ds(h * BLOCK, BLOCK)] = att_stack[0, h, pl.ds(0, TOK), :].astype(F32)
    roll_out(3, tmp_f, False)
    gather(6, 7)
    att_grad(g_stack.at[1], 1)
    attend_back(1, 0, 4)
    turn_att(1)
    reduce_1(1)
    mid_f[pl.ds(0, QUARTER), :] = tmp_f[pl.ds(3 * QUARTER, QUARTER), :]
    for i in range(3):
        mid_f[pl.ds((i + 1) * QUARTER, QUARTER), :] = roll_in(3, i)
    for h in range(4):
        att_stack[2, h, pl.ds(0, TOK), :] = mid_f[:, pl.ds(h * BLOCK, BLOCK)].astype(BF16)
    send_att(2)
    attend_back(1, 4, 8)
    turn_att(2)
    normed_grad(1)
    mid_f[...] = norm_back(sh_f[...], gain2_ref[...], tmp_f[...])
    g_stack[2, pl.ds(0, TOK), :] = mid_f[...].astype(BF16)
    send_grad(2)
    roll_out(2, mid_f, True)
    reduce_1(0)
    sh_f[pl.ds(3 * QUARTER, QUARTER), :] = mid_f[pl.ds(0, QUARTER), :].astype(BF16).astype(F32)
    for i, quarter in enumerate((2, 1, 0)):
        sh_f[pl.ds(quarter * QUARTER, QUARTER), :] = roll_in(2, i)
    mid_f[...] = (go_f[...] + sh_f[...]).astype(BF16).astype(F32)
    norm_buf[...] = mid_f[...].astype(BF16)
    att_grad(norm_buf, 0)
    reduce_2(1)
    attend_back(0)
    reduce_3(1)
    normed_grad(0)
    reduce_2(0)
    sh_f[...] = mid_f[...] + norm_back(tok_f[...], gain1_ref[...], tmp_f[...]).astype(BF16).astype(F32)
    for r in range(WIN):
        rows = jnp.concatenate(
            [sh_f[pl.ds(r * HALF, HALF), :], sh_f[pl.ds(72 + r * HALF, HALF), :]], axis=0)
        out_ref[0, r] = rows.astype(BF16)
    reduce_3(0)
    reduce_4(1)
    reduce_4(0)
    reduce_end(1, og2_ref)
    reduce_end(0, og1_ref)
    for group_of in (flights, rolls, sibs):
        for c in group_of.values():
            c.wait_send()
    for some in steps.values():
        for c in some:
            c.wait_send()


def on_device(
    tokens, grad_out, first_gain, first_qkv_weight, first_out_weight, first_bias,
    second_gain, second_qkv_weight, second_out_weight, second_bias, rel_index, classes,
):
    vmem = pl.BlockSpec(memory_space=pltpu.VMEM)
    hbm = pl.BlockSpec(memory_space=pl.ANY)
    dma = pltpu.SemaphoreType.DMA
    return pl.pallas_call(
        kernel,
        out_shape=(
            jax.ShapeDtypeStruct((1, WIN, WIN, D), BF16),
            jax.ShapeDtypeStruct((16, D), F32),
            jax.ShapeDtypeStruct((16, D), F32),
        ),
        in_specs=[hbm] * 2 + [vmem] * 2 + [hbm] * 8,
        out_specs=(vmem, vmem, vmem),
        scratch_shapes=[
            pltpu.VMEM((1, WIN, WIN, D), BF16),
            pltpu.VMEM((1, WIN, WIN, D), BF16),
            pltpu.VMEM(first_bias.shape[::-1], F32),
            pltpu.VMEM(second_bias.shape[::-1], F32),
            pltpu.VMEM((TOK, TOK), jnp.int32),
            pltpu.VMEM((WIN, WIN), jnp.int32),
            pltpu.VMEM((2 * HEADS, TABLE), F32),
            pltpu.VMEM((8, NY, 2, 2, NZ, 2, 16, BLOCK), BF16),
            pltpu.VMEM((2 * HEADS, TOK, TOK), F32),
            pltpu.VMEM((16, 512), jnp.int32),
            pltpu.VMEM((WIN, 2 * HEADS, 512), F32),
            pltpu.VMEM((2 * HEADS, 16, 512), F32),
            pltpu.VMEM((TOK, TOK), F32),
            pltpu.VMEM((2 * HEADS, TOK, TOK), BF16),
            pltpu.VMEM((2, TOK, 3 * D), BF16),
            pltpu.VMEM((TOK, 3 * D), BF16),
            pltpu.VMEM((TOK, D), BF16),
            pltpu.VMEM((TOK, D), BF16),
            pltpu.VMEM((TOK, D), F32),
            pltpu.VMEM((TOK, D), F32),
            pltpu.VMEM((TOK, D), F32),
            pltpu.VMEM((TOK, D), F32),
            pltpu.VMEM((TOK, D), F32),
            pltpu.VMEM((3, 2 * TOK, D), BF16),
            pltpu.VMEM((3, 4, 2 * TOK, BLOCK), BF16),
            pltpu.VMEM((4, 3, TOK, BLOCK), BF16),
            pltpu.VMEM((4, 3, TOK, BLOCK), BF16),
            pltpu.VMEM((3, TOK, D), F32),
            pltpu.VMEM((3, 2, BLOCK, 2 * TOK), BF16),
            pltpu.VMEM((2, BLOCK, D), F32),
            pltpu.VMEM((2, 2, NZ, 2, 16, 512), BF16),
            pltpu.VMEM((2, NX - 1, NZ, 16, 512), BF16),
            pltpu.VMEM((2, NZ, 16, 512), BF16),
            pltpu.VMEM((2, NZ - 1, 16, 512), BF16),
            pltpu.VMEM((2, NY, 16, 512), BF16),
            pltpu.VMEM((2, NY, 2, NZ, 2, 16, 128), BF16),
            pltpu.VMEM((2, NY - 1, 2, NZ, 2, 16, 128), BF16),
            pltpu.VMEM((2, 2, NZ, 2, 16, 128), BF16),
            pltpu.VMEM((2, NX - 1, NZ, 16, 128), BF16),
            pltpu.VMEM((2, NZ, 16, 128), BF16),
            pltpu.VMEM((2, NZ - 1, 16, 128), BF16),
            pltpu.VMEM((2, NY, 16, 128), BF16),
            dma((6,)),
            dma((8,)),
            dma((8, 24)), dma((8, 24)),
            dma((4, 3)), dma((4, 3)),
            dma((9,)), dma((9,)),
            dma((2, 29)), dma((2, 29)),
        ],
        compiler_params=pltpu.CompilerParams(
            collective_id=0, has_side_effects=True, vmem_limit_bytes=56 * 1024 * 1024
        ),
        name="window_blocks",
    )(
        tokens, grad_out, first_gain[None], second_gain[None],
        first_qkv_weight, first_out_weight, second_qkv_weight, second_out_weight,
        first_bias.T, second_bias.T, rel_index, classes,
    )


def solution(mesh):
    tile = P("rep", "lat", "lon", None)
    rows = P(("lat", "lon"), None)
    in_specs = (tile, tile, P(), rows, rows, P(), P(), rows, rows, P(), P(), P("lat", "lon"))
    return jax.shard_map(
        on_device, mesh=mesh, in_specs=in_specs, out_specs=(tile, rows, rows), check_vma=False
    )
```

```python
import jax
import jax.numpy as jnp
from jax import lax
from jax.experimental import pallas as pl
from jax.experimental.pallas import tpu as pltpu
from jax.sharding import PartitionSpec as P

HEADS = 16
WIN = 12
HALF = WIN // 2
TOK = WIN * WIN
QUARTER = HALF * HALF
D = 1024
EPSILON = 1e-05
NX, NY, NZ = 4, 4, 8
TABLE = 640
BLOCK = 256
LOW = -1e30
MESH = pl.DeviceIdType.MESH
F32 = jnp.float32
BF16 = jnp.bfloat16

ORDERS = ("zxy", "zyx", "xyz", "zxy", "zyx", "zxy", "xyz", "zyx")
STAGES = 7


def dot(a, b):
    return jnp.dot(a, b, preferred_element_type=F32)


def dot_t(a, b):
    return lax.dot_general(a, b, (((1,), (1,)), ((), ())), preferred_element_type=F32)


def t_dot(a, b):
    return lax.dot_general(a, b, (((0,), (0,)), ((), ())), preferred_element_type=F32)


def iota(shape, dim):
    return lax.broadcasted_iota(jnp.int32, shape, dim)


def over_six(n):
    return (n * 10923) >> 16


def qkv_column(n):
    return (n % 3) * D + (n // 3) * BLOCK


def norm_parts(x):
    centered = x - jnp.mean(x, axis=-1, keepdims=True)
    scale = lax.rsqrt(jnp.mean(centered * centered, axis=-1, keepdims=True) + EPSILON)
    return centered * scale, scale


def norm_back(x, gain, grad):
    unit, scale = norm_parts(x)
    g = grad * gain
    return scale * (
        g - jnp.mean(g, axis=-1, keepdims=True) - unit * jnp.mean(g * unit, axis=-1, keepdims=True)
    )


def kernel(
    tokens_ref, grad_ref, gain1_ref, gain2_ref, wq1_ref, wo1_ref, wq2_ref, wo2_ref,
    bias1_ref, bias2_ref, rel_in, cls_in,
    out_ref, og1_ref, og2_ref,
    tokens_v, grad_v, bias1_v, bias2_v, rel_ref, cls_ref, tab,
    wbuf, bias, idx_u, u_raw, u_ref, same, probs, qkv, dqkv, norm_buf, datt,
    tok_f, go_f, mid_f, sh_f, tmp_f, g_stack, att_stack, roll_s, roll_r,
    partial, att_t, early, xs, xr, zs, zr, ys, vs, vr, ws, wr, us, ur, os,
    load_sem, w_local, w_send, w_recv, roll_send, roll_recv, sib_send, sib_recv, red_send, red_recv,
):
    lat, lon, y = lax.axis_index("lat"), lax.axis_index("lon"), lax.axis_index("rep")
    xh, core = lat // 2, lat % 2
    z, xl = lon // 2, lon % 2
    x = xh * 2 + xl
    other = 1 - core

    def at_x(d):
        n = (x + d) % NX
        return ((n // 2) * 2 + core, z * 2 + n % 2, y)

    def at_z(d):
        return (lat, ((z + d) % NZ) * 2 + xl, y)

    def at_y(d):
        return (lat, lon, (y + d) % NY)

    sibling = (xh * 2 + other, lon, y)

    def at_roll(a, b):
        return ((lat + a + 4) % 4, (lon + b + 16) % 16, y)

    def copy(src, dst, send, recv, device):
        return pltpu.make_async_remote_copy(
            src_ref=src, dst_ref=dst, send_sem=send, recv_sem=recv,
            device_id=device, device_id_type=MESH,
        )

    barrier = pltpu.get_barrier_semaphore()
    partners = [at_z(d) for d in range(1, NZ)] + [at_x(d) for d in range(1, NX)]
    partners += [at_y(d) for d in range(1, NY)] + [sibling]
    partners += [at_roll(*s) for s in ((1, 0), (-1, 0), (0, 1), (0, -1), (1, 1), (-1, -1))]
    for partner in partners:
        pl.semaphore_signal(barrier, inc=1, device_id=partner, device_id_type=MESH)
    local = []
    for u in range(8):
        source = (wq1_ref, wo1_ref, wq2_ref, wo2_ref)[(u // 4) * 2 + (u % 4) // 3]
        n = (u % 4) * 4 + y
        column = qkv_column(n) if u % 4 < 3 else y * BLOCK
        local.append(
            pltpu.make_async_copy(
                source.at[:, pl.ds(pl.multiple_of(column, BLOCK), BLOCK)],
                wbuf.at[u, y, xh, core, z, xl], w_local.at[u],
            )
        )
        local[-1].start()

    loads = [
        pltpu.make_async_copy(source, target, load_sem.at[i])
        for i, (source, target) in enumerate((
            (grad_ref, grad_v), (rel_in, rel_ref), (tokens_ref, tokens_v),
            (bias1_ref, bias1_v), (bias2_ref, bias2_v), (cls_in, cls_ref)))
    ]
    for c in loads:
        c.start()

    pl.semaphore_wait(barrier, len(partners))
    for c in local:
        c.wait()

    flights, counts = {}, [0] * 8

    def send(u, tag, src, device):
        k = counts[u]
        counts[u] += 1
        c = copy(src, src, w_send.at[u, k], w_recv.at[u, k], device)
        c.start()
        flights[u, k] = c
        waits.setdefault((u, tag), []).append(c)

    waits = {}

    def got(u, tag):
        for c in waits[u, tag]:
            c.wait_recv()

    def element(u):
        return wbuf.at[u, y, xh, core, z, xl]

    def wrap(n, size):
        return (n + size) % size

    def spread(u, tag, src, at, size):
        for d in sorted(range(1, size), key=lambda d: -min(d, size - d)):
            send(u, tag, src, at(d))

    def share(u, src):
        send(u, "share", src, sibling)

    def stage_zxy(u, stage):
        def plane(d):
            return wbuf.at[u, wrap(y + d, NY), :, core]

        def half(d, h):
            return wbuf.at[u, wrap(y + d, NY), h, core]

        if stage == 0:
            spread(u, 0, element(u), at_z, NZ)
        if stage == 1:
            got(u, 0)
            spread(u, 1, wbuf.at[u, y, xh, core, :, xl], at_x, NX)
        if stage == 2:
            got(u, 1)
            send(u, "r1", half(0, 0), at_y(1))
            send(u, "l1", half(0, 1), at_y(3))
            send(u, "r2", half(0, 1), at_y(1))
            send(u, "l2", half(0, 0), at_y(3))
            share(u, plane(0))
        if stage == 3:
            got(u, "r1")
            send(u, "far", half(-1, 0), at_y(1))
            got(u, "l1")
            send(u, "far", half(1, 1), at_y(3))
        if stage == 4:
            got(u, "r2")
            share(u, plane(-1))
            got(u, "l2")
            share(u, plane(1))
        if stage == 5:
            got(u, "far")
            share(u, plane(2))

    def stage_zyx(u, stage):
        def column(d):
            n = wrap(x + d, NX)
            return wbuf.at[u, :, n // 2, core, :, n % 2]

        def half(d, h):
            n = wrap(x + d, NX)
            return wbuf.at[u, pl.ds(2 * h, 2), n // 2, core, :, n % 2]

        if stage == 0:
            spread(u, 0, element(u), at_z, NZ)
        if stage == 1:
            got(u, 0)
            spread(u, 1, wbuf.at[u, y, xh, core, :, xl], at_y, NY)
        if stage == 2:
            got(u, 1)
            send(u, "r1", half(0, 0), at_x(1))
            send(u, "l1", half(0, 1), at_x(3))
            send(u, "r2", half(0, 1), at_x(1))
            send(u, "l2", half(0, 0), at_x(3))
            share(u, column(0))
        if stage == 3:
            got(u, "r1")
            send(u, "far", half(-1, 0), at_x(1))
            got(u, "l1")
            send(u, "far", half(1, 1), at_x(3))
        if stage == 4:
            got(u, "r2")
            share(u, column(-1))
            got(u, "l2")
            share(u, column(1))
        if stage == 5:
            got(u, "far")
            share(u, column(2))

    def stage_xyz(u, stage):
        def group(d):
            return wbuf.at[u, :, :, core, wrap(z + d, NZ)]

        def half(d, h):
            return wbuf.at[u, pl.ds(2 * h, 2), :, core, wrap(z + d, NZ)]

        if stage == 0:
            spread(u, 0, element(u), at_x, NX)
        if stage == 1:
            got(u, 0)
            spread(u, 1, wbuf.at[u, y, :, core, z], at_y, NY)
        if stage == 2:
            got(u, 1)
            send(u, "r2", group(0), at_z(2))
            send(u, "l2", group(0), at_z(6))
            send(u, "r1", group(0), at_z(1))
            send(u, "l1", group(0), at_z(7))
            share(u, group(0))
        if stage == 3:
            got(u, "r2")
            send(u, "far", half(-2, 0), at_z(2))
            send(u, "far", group(-2), at_z(1))
            got(u, "l2")
            send(u, "far", half(2, 1), at_z(6))
            send(u, "far", group(2), at_z(7))
        if stage == 4:
            got(u, "r1")
            got(u, "l1")
            for d in (-2, -1, 1, 2):
                share(u, group(d))
        if stage == 5:
            got(u, "far")
            for d in (-3, 3, 4):
                share(u, group(d))

    def gather_stage(u, stage):
        if 0 <= stage < STAGES:
            {"zxy": stage_zxy, "zyx": stage_zyx, "xyz": stage_xyz}[ORDERS[u]](u, stage)
        if stage == 6:
            got(u, "share")

    def gather(stage, *units):
        for u in units:
            gather_stage(u, stage)

    gather(0, 0, 1, 2, 3, 4, 5, 6, 7)
    for c in loads:
        c.wait()

    for r in range(WIN):
        for source, target in ((tokens_v, tok_f), (grad_v, go_f)):
            rows = source[0, r].astype(F32)
            target[pl.ds(r * HALF, HALF), :] = rows[:HALF]
            target[pl.ds(72 + r * HALF, HALF), :] = rows[HALF:]

    rolls = {}

    def roll_out(which, source, back):
        to = 1 if back else -1
        places = ((1, (to, 0)), (2, (0, to)), (3, (to, to))) if back else (
            (2, (to, 0)), (1, (0, to)), (0, (to, to)))
        for i, (quarter, shift) in enumerate(places):
            rows = source[pl.ds(quarter * QUARTER, QUARTER), :]
            roll_s[which, i] = jnp.concatenate(
                [rows[:, c * BLOCK:(c + 1) * BLOCK] for c in range(4)], axis=0).astype(BF16)
            c = copy(roll_s.at[which, i], roll_r.at[which, i],
                     roll_send.at[which, i], roll_recv.at[which, i], at_roll(*shift))
            c.start()
            rolls[which, i] = c

    def roll_in(which, i):
        rolls[which, i].wait_recv()
        rows = roll_r[which, i].astype(F32)
        return jnp.concatenate(
            [rows[c * QUARTER:(c + 1) * QUARTER] for c in range(4)], axis=1)


    k_of = iota((TOK, 512), 0)
    lane = iota((TOK, 512), 1)
    side = (lane >= 256).astype(jnp.int32)
    j = lane - side * (256 + 72)
    s = over_six(jnp.maximum(j, 0))
    c = side * HALF + j - s * HALF
    inside = (j >= 0) & (j < 138)
    late = s > 11
    wanted = jnp.where(late, s - 11, s) * WIN + c
    hit = inside & (k_of == wanted)
    pick_a = jnp.where(hit & (s <= 11), 1.0, 0.0).astype(BF16)
    pick_b = jnp.where(hit & late, 1.0, 0.0).astype(BF16)
    high_a = dot((rel_ref[pl.ds(TOK - WIN, WIN), :] >> 4).astype(F32).astype(BF16), pick_a)
    low_a = dot((rel_ref[pl.ds(TOK - WIN, WIN), :] & 15).astype(F32).astype(BF16), pick_a)
    high_b = dot((rel_ref[pl.ds(0, WIN), :] >> 4).astype(F32).astype(BF16), pick_b)
    low_b = dot((rel_ref[pl.ds(0, WIN), :] & 15).astype(F32).astype(BF16), pick_b)
    idx_u[pl.ds(0, WIN), :] = ((high_a + high_b) * 16.0 + low_a + low_b).astype(jnp.int32)
    gather(1, 0, 1, 2)

    tab[...] = jnp.zeros_like(tab)
    entries = bias1_v.shape[1]
    tab[pl.ds(0, HEADS), pl.ds(0, entries)] = bias1_v[...]
    tab[pl.ds(HEADS, HEADS), pl.ds(0, entries)] = bias2_v[...]
    table = tab[...]
    t_high = table.astype(BF16)
    rest = table - t_high.astype(F32)
    t_mid = rest.astype(BF16)
    t_low = (rest - t_mid.astype(F32)).astype(BF16)
    parts = jnp.concatenate([t_high, t_mid, t_low], axis=0)

    def choose(c1, _):
        chosen = idx_u[pl.ds(c1, 1), :]
        onehot = jnp.where(iota((TABLE, 512), 0) == chosen, 1.0, 0.0).astype(BF16)
        got3 = dot(parts, onehot)
        u_raw[c1] = got3[0:32] + got3[32:64] + got3[64:96]
        return 0

    lax.fori_loop(0, WIN, choose, 0)
    gather(2, 0, 1, 2)
    gather(1, 3, 4, 6, 5, 7)
    for th in range(2 * HEADS):
        rows = u_raw[:, th, :]
        u_ref[th, pl.ds(0, HALF), :] = rows[:HALF]
        u_ref[th, pl.ds(8, HALF), :] = rows[HALF:]

    def slide(th, _):
        left, right = u_ref[th, :, pl.ds(0, 256)], u_ref[th, :, pl.ds(256, 256)]
        first = iota((16, 256), 1) < 72
        for r in range(WIN):
            shift = (256 - HALF * (11 - r)) % 256
            a = pltpu.roll(left, shift, 1) if shift else left
            b = pltpu.roll(right, shift, 1) if shift else right
            value = jnp.where(first, a, b)[:, :TOK]
            bias[th, pl.ds(r * HALF, HALF), :] = value[:HALF]
            bias[th, pl.ds(72 + r * HALF, HALF), :] = value[8:8 + HALF]
        return 0

    lax.fori_loop(0, HEADS, slide, 0)

    n = iota((TOK, WIN), 0)
    right_half = (n >= 72).astype(jnp.int32)
    n = n - 72 * right_half
    row_of = over_six(n)
    col_of = right_half * HALF + n - row_of * HALF
    row_pick = jnp.where(iota((TOK, WIN), 1) == row_of, 1.0, 0.0).astype(BF16)
    per_row = dot(row_pick, cls_ref[...].astype(F32).astype(BF16))
    label = jnp.sum(
        jnp.where(iota((TOK, WIN), 1) == col_of, per_row, 0.0), axis=1, keepdims=True)
    member = jnp.where(iota((TOK, 128), 1) == label.astype(jnp.int32), 1.0, 0.0).astype(BF16)
    same[...] = dot_t(member, member)

    gather(3, 0, 1)
    gather(2, 3, 4)
    lax.fori_loop(HEADS, 2 * HEADS, slide, 0)

    even = jnp.where(iota((1, 128), 1) < 64, 1.0, 0.0).astype(BF16)
    masks = (even, (1.0 - even.astype(F32)).astype(BF16))

    def weight(u, block):
        return wbuf[u, block].reshape(D, BLOCK)

    def times_rows(left, u, block):
        result = None
        for c in range(4):
            term = dot_t(left(c), wbuf[u, c, block // 2, block % 2].reshape(BLOCK, BLOCK))
            result = term if result is None else result + term
        return result

    def project(which, own, *parts_of):
        half = core if own else other
        for u in parts_of:
            for i in range(4):
                cols = pl.ds(i * BLOCK, BLOCK)
                result = None if own else partial[u, :, cols]
                for h in range(2):
                    rows = pl.ds(pl.multiple_of(h * 512 + half * BLOCK, BLOCK), BLOCK)
                    term = dot(norm_buf[:, rows], wbuf[which * 4 + u, i, h, half].reshape(BLOCK, BLOCK))
                    result = term if result is None else result + term
                if own:
                    partial[u, :, cols] = result
                else:
                    qkv[which, :, pl.ds(qkv_column(u * 4 + i), BLOCK)] = result.astype(BF16)

    def lanes(i, offset=0):
        return pl.ds(pl.multiple_of(offset + i * 128, 128), 128)

    def attend(which, first=0, last=HEADS // 2):
        def step(i, _):
            q2 = qkv[which, :, lanes(i)]
            k2 = qkv[which, :, lanes(i, D)]
            v2 = qkv[which, :, lanes(i, 2 * D)]
            mixed = None
            for e in range(2):
                score = dot_t(q2 * masks[e], k2) * 0.125 + bias[which * HEADS + 2 * i + e]
                if which:
                    score = jnp.where(same[...] > 0.5, score, LOW)
                power = jnp.exp(score - jnp.max(score, axis=1, keepdims=True))
                share_of = (power * (1.0 / jnp.sum(power, axis=1, keepdims=True))).astype(BF16)
                probs[which * HEADS + 2 * i + e] = share_of
                term = dot(share_of, v2 * masks[e])
                mixed = term if mixed is None else mixed + term
            att_stack[which, i // 2, pl.ds(0, TOK), lanes(i % 2)] = mixed.astype(BF16)
            return 0
        lax.fori_loop(first, last, step, 0, unroll=4)

    def attend_back(which, first=0, last=HEADS // 2):
        def step(i, _):
            q2 = qkv[which, :, lanes(i)]
            k2 = qkv[which, :, lanes(i, D)]
            v2 = qkv[which, :, lanes(i, 2 * D)]
            do2 = datt[:, lanes(i)]
            dq = dk = dv = None
            for e in range(2):
                share_of = probs[which * HEADS + 2 * i + e]
                up = do2 * masks[e]
                dp = dot_t(up, v2)
                share_f = share_of.astype(F32)
                mean = jnp.sum(dp * share_f, axis=1, keepdims=True)
                ds = (share_f * (dp - mean) * 0.125).astype(BF16)
                a = t_dot(share_of, up)
                b = dot(ds, k2 * masks[e])
                c = t_dot(ds, q2 * masks[e])
                dv = a if dv is None else dv + a
                dq = b if dq is None else dq + b
                dk = c if dk is None else dk + c
            dqkv[:, lanes(i)] = dq.astype(BF16)
            dqkv[:, lanes(i, D)] = dk.astype(BF16)
            dqkv[:, lanes(i, 2 * D)] = dv.astype(BF16)
            return 0
        lax.fori_loop(first, last, step, 0, unroll=4)

    def att_grad(source, which):
        for b in range(4):
            datt[:, pl.ds(b * BLOCK, BLOCK)] = times_rows(
                lambda c: source[pl.ds(0, TOK), pl.ds(c * BLOCK, BLOCK)],
                which * 4 + 3, b).astype(BF16)

    def normed_grad(which):
        for b in range(4):
            result = None
            for u in range(3):
                term = times_rows(
                    lambda c: dqkv[:, pl.ds(qkv_column(u * 4 + c), BLOCK)], which * 4 + u, b)
                result = term if result is None else result + term
            tmp_f[:, pl.ds(b * BLOCK, BLOCK)] = result.astype(BF16).astype(F32)

    sibs = {}

    def to_sibling(name, k, src, dst):
        c = copy(src, dst, sib_send.at[k], sib_recv.at[k], sibling)
        c.start()
        sibs[name] = c

    def send_att(m):
        for h in range(2):
            to_sibling((m, h), m * 3 + h, att_stack.at[m, h * 2 + other, pl.ds(0, TOK)],
                       att_stack.at[m, h * 2 + other, pl.ds(TOK, TOK)])

    def send_grad(m):
        to_sibling((m, 2), m * 3 + 2, g_stack.at[m, pl.ds(0, TOK)], g_stack.at[m, pl.ds(TOK, TOK)])

    def turn_att(m):
        for h in range(2):
            sibs[m, h].wait_recv()
            att_t[m, h] = att_stack[m, h * 2 + core].astype(F32).T.astype(BF16)

    steps = {}

    def ship(m, name, k, src, dst, device):
        c = copy(src, dst, red_send.at[m, k], red_recv.at[m, k], device)
        c.start()
        steps.setdefault((m, name), []).append(c)

    def landed(m, name):
        for c in steps[m, name]:
            c.wait_recv()

    def product(m, h, cols):
        return dot(att_t[m, h], g_stack[m, :, cols])

    def early_product():
        sibs[0, 2].wait_recv()
        for h in range(2):
            for c in range(4):
                cols = pl.ds(c * BLOCK, BLOCK)
                early[h, :, cols] = product(0, h, cols)

    def reduce_1(m):
        sibs[2 if m == 0 else 1, 2].wait_recv()
        for h in range(2):
            for c in range(4):
                cols = pl.ds(c * BLOCK, BLOCK)
                if m == 0:
                    value = product(2, h, cols) + early[h, :, cols]
                else:
                    value = product(1, h, cols)
                value = value.astype(BF16)
                if c < 2:
                    xs[m, h, :, :, :, cols] = value.reshape(NZ, 2, 16, BLOCK)
                else:
                    for q in range(2):
                        vs[m, (c - 2) * 2 + q, h] = value[:, q * 128:(q + 1) * 128].reshape(
                            NZ, 2, 16, 128)
        for d in (2, 1, 3):
            target = (x + d) % NX
            ship(m, "xx", d - 1, xs.at[m, target // 2, :, target % 2], xr.at[m, d - 1], at_x(d))
            ship(m, "vy", 2 + d, vs.at[m, (y + d) % NY], vr.at[m, d - 1], at_y(d))

    def reduce_2(m):
        landed(m, "xx")
        value = xs[m, xh, :, xl].astype(F32)
        for d in range(NX - 1):
            value = value + xr[m, d].astype(F32)
        zs[m] = value.astype(BF16)
        for d in (4, 3, 5, 2, 6, 1, 7):
            ship(m, "xz", 5 + d, zs.at[m, (z + d) % NZ], zr.at[m, d - 1], at_z(d))
        landed(m, "vy")
        value = vs[m, y].astype(F32)
        for d in range(NY - 1):
            value = value + vr[m, d].astype(F32)
        ws[m] = value.astype(BF16)
        for d in (2, 1, 3):
            target = (x + d) % NX
            ship(m, "vx", 12 + d, ws.at[m, target // 2, :, target % 2], wr.at[m, d - 1], at_x(d))

    def reduce_3(m):
        landed(m, "vx")
        value = ws[m, xh, :, xl].astype(F32)
        for d in range(NX - 1):
            value = value + wr[m, d].astype(F32)
        us[m] = value.astype(BF16)
        for d in (4, 3, 5, 2, 6, 1, 7):
            ship(m, "vz", 15 + d, us.at[m, (z + d) % NZ], ur.at[m, d - 1], at_z(d))
        landed(m, "xz")
        value = zs[m, z].astype(F32)
        for d in range(NZ - 1):
            value = value + zr[m, d].astype(F32)
        ys[m, y] = value.astype(BF16)
        for d in range(1, NY):
            ship(m, "xy", 22 + d, ys.at[m, y], ys.at[m, y], at_y(d))

    def reduce_4(m):
        landed(m, "vz")
        value = us[m, z].astype(F32)
        for d in range(NZ - 1):
            value = value + ur[m, d].astype(F32)
        os[m, y] = value.astype(BF16)
        for d in range(1, NY):
            ship(m, "vo", 25 + d, os.at[m, y], os.at[m, y], at_y(d))

    def reduce_end(m, target):
        landed(m, "xy")
        value = ys[m, 0].astype(F32)
        for i in range(1, NY):
            value = value + ys[m, i].astype(F32)
        target[:, pl.ds(0, 512)] = value
        landed(m, "vo")
        for i in range(NY):
            target[:, pl.ds(512 + i * 128, 128)] = os[m, i].astype(F32)

    gather(3, 2)
    gather(2, 6)
    gather(4, 0, 1)
    unit, _ = norm_parts(tok_f[...])
    norm_buf[...] = (unit * gain1_ref[...]).astype(BF16)
    g_stack[0, pl.ds(0, TOK), :] = go_f[...].astype(BF16)
    send_grad(0)
    gather(5, 0, 1)
    gather(4, 2)
    project(0, True, 0, 1)
    gather(3, 3, 4)
    gather(2, 5, 7)
    gather(6, 0, 1)
    project(0, False, 0, 1)
    gather(5, 2)
    attend(0, 0, 4)
    gather(4, 3, 4)
    project(0, True, 2)
    gather(6, 2)
    project(0, False, 2)
    gather(5, 3, 4)
    attend(0, 4, 8)
    send_att(0)
    gather(3, 5, 7)
    gather(3, 6)
    gather(6, 3)
    for b in range(4):
        cols = pl.ds(b * BLOCK, BLOCK)
        result = tok_f[:, cols]
        for h in range(4):
            result = result + dot(att_stack[0, h, pl.ds(0, TOK), :],
                                  wbuf[3, b, h // 2, h % 2].reshape(BLOCK, BLOCK))
        mid_f[:, cols] = result.astype(BF16).astype(F32)
    roll_out(1, mid_f, False)
    roll_out(0, go_f, False)
    turn_att(0)
    gather(4, 5, 7)
    gather(4, 6)
    early_product()
    gather(6, 4)
    gather(5, 5, 7)
    sh_f[pl.ds(0, QUARTER), :] = mid_f[pl.ds(3 * QUARTER, QUARTER), :]
    for i in range(3):
        sh_f[pl.ds((i + 1) * QUARTER, QUARTER), :] = roll_in(1, i)
    unit, _ = norm_parts(sh_f[...])
    norm_buf[...] = (unit * gain2_ref[...]).astype(BF16)
    project(1, True, 0)
    project(1, False, 0)
    project(1, True, 1)
    gather(6, 5)
    project(1, False, 1)
    gather(5, 6)
    project(1, True, 2)
    attend(1, 0, 4)
    mid_f[pl.ds(0, QUARTER), :] = go_f[pl.ds(3 * QUARTER, QUARTER), :]
    for i in range(3):
        mid_f[pl.ds((i + 1) * QUARTER, QUARTER), :] = roll_in(0, i)
    g_stack[1, pl.ds(0, TOK), :] = mid_f[...].astype(BF16)
    send_grad(1)
    gather(6, 6)
    project(1, False, 2)
    attend(1, 4, 8)
    send_att(1)
    for h in range(4):
        tmp_f[:, pl.ds(h * BLOCK, BLOCK)] = att_stack[0, h, pl.ds(0, TOK), :].astype(F32)
    roll_out(3, tmp_f, False)
    gather(6, 7)
    att_grad(g_stack.at[1], 1)
    attend_back(1, 0, 4)
    turn_att(1)
    reduce_1(1)
    mid_f[pl.ds(0, QUARTER), :] = tmp_f[pl.ds(3 * QUARTER, QUARTER), :]
    for i in range(3):
        mid_f[pl.ds((i + 1) * QUARTER, QUARTER), :] = roll_in(3, i)
    for h in range(4):
        att_stack[2, h, pl.ds(0, TOK), :] = mid_f[:, pl.ds(h * BLOCK, BLOCK)].astype(BF16)
    send_att(2)
    attend_back(1, 4, 8)
    turn_att(2)
    normed_grad(1)
    mid_f[...] = norm_back(sh_f[...], gain2_ref[...], tmp_f[...])
    g_stack[2, pl.ds(0, TOK), :] = mid_f[...].astype(BF16)
    send_grad(2)
    roll_out(2, mid_f, True)
    reduce_1(0)
    sh_f[pl.ds(3 * QUARTER, QUARTER), :] = mid_f[pl.ds(0, QUARTER), :].astype(BF16).astype(F32)
    for i, quarter in enumerate((2, 1, 0)):
        sh_f[pl.ds(quarter * QUARTER, QUARTER), :] = roll_in(2, i)
    mid_f[...] = (go_f[...] + sh_f[...]).astype(BF16).astype(F32)
    norm_buf[...] = mid_f[...].astype(BF16)
    att_grad(norm_buf, 0)
    reduce_2(1)
    attend_back(0)
    reduce_3(1)
    normed_grad(0)
    reduce_2(0)
    sh_f[...] = mid_f[...] + norm_back(tok_f[...], gain1_ref[...], tmp_f[...]).astype(BF16).astype(F32)
    for r in range(WIN):
        rows = jnp.concatenate(
            [sh_f[pl.ds(r * HALF, HALF), :], sh_f[pl.ds(72 + r * HALF, HALF), :]], axis=0)
        out_ref[0, r] = rows.astype(BF16)
    reduce_3(0)
    reduce_4(1)
    reduce_4(0)
    reduce_end(1, og2_ref)
    reduce_end(0, og1_ref)
    for group_of in (flights, rolls, sibs):
        for c in group_of.values():
            c.wait_send()
    for some in steps.values():
        for c in some:
            c.wait_send()


def on_device(
    tokens, grad_out, first_gain, first_qkv_weight, first_out_weight, first_bias,
    second_gain, second_qkv_weight, second_out_weight, second_bias, rel_index, classes,
):
    vmem = pl.BlockSpec(memory_space=pltpu.VMEM)
    hbm = pl.BlockSpec(memory_space=pl.ANY)
    dma = pltpu.SemaphoreType.DMA
    return pl.pallas_call(
        kernel,
        out_shape=(
            jax.ShapeDtypeStruct((1, WIN, WIN, D), BF16),
            jax.ShapeDtypeStruct((16, D), F32),
            jax.ShapeDtypeStruct((16, D), F32),
        ),
        in_specs=[hbm] * 2 + [vmem] * 2 + [hbm] * 8,
        out_specs=(vmem, vmem, vmem),
        scratch_shapes=[
            pltpu.VMEM((1, WIN, WIN, D), BF16),
            pltpu.VMEM((1, WIN, WIN, D), BF16),
            pltpu.VMEM(first_bias.shape[::-1], F32),
            pltpu.VMEM(second_bias.shape[::-1], F32),
            pltpu.VMEM((TOK, TOK), jnp.int32),
            pltpu.VMEM((WIN, WIN), jnp.int32),
            pltpu.VMEM((2 * HEADS, TABLE), F32),
            pltpu.VMEM((8, NY, 2, 2, NZ, 2, 16, BLOCK), BF16),
            pltpu.VMEM((2 * HEADS, TOK, TOK), F32),
            pltpu.VMEM((16, 512), jnp.int32),
            pltpu.VMEM((WIN, 2 * HEADS, 512), F32),
            pltpu.VMEM((2 * HEADS, 16, 512), F32),
            pltpu.VMEM((TOK, TOK), F32),
            pltpu.VMEM((2 * HEADS, TOK, TOK), BF16),
            pltpu.VMEM((2, TOK, 3 * D), BF16),
            pltpu.VMEM((TOK, 3 * D), BF16),
            pltpu.VMEM((TOK, D), BF16),
            pltpu.VMEM((TOK, D), BF16),
            pltpu.VMEM((TOK, D), F32),
            pltpu.VMEM((TOK, D), F32),
            pltpu.VMEM((TOK, D), F32),
            pltpu.VMEM((TOK, D), F32),
            pltpu.VMEM((TOK, D), F32),
            pltpu.VMEM((3, 2 * TOK, D), BF16),
            pltpu.VMEM((3, 4, 2 * TOK, BLOCK), BF16),
            pltpu.VMEM((4, 3, TOK, BLOCK), BF16),
            pltpu.VMEM((4, 3, TOK, BLOCK), BF16),
            pltpu.VMEM((3, TOK, D), F32),
            pltpu.VMEM((3, 2, BLOCK, 2 * TOK), BF16),
            pltpu.VMEM((2, BLOCK, D), F32),
            pltpu.VMEM((2, 2, NZ, 2, 16, 512), BF16),
            pltpu.VMEM((2, NX - 1, NZ, 16, 512), BF16),
            pltpu.VMEM((2, NZ, 16, 512), BF16),
            pltpu.VMEM((2, NZ - 1, 16, 512), BF16),
            pltpu.VMEM((2, NY, 16, 512), BF16),
            pltpu.VMEM((2, NY, 2, NZ, 2, 16, 128), BF16),
            pltpu.VMEM((2, NY - 1, 2, NZ, 2, 16, 128), BF16),
            pltpu.VMEM((2, 2, NZ, 2, 16, 128), BF16),
            pltpu.VMEM((2, NX - 1, NZ, 16, 128), BF16),
            pltpu.VMEM((2, NZ, 16, 128), BF16),
            pltpu.VMEM((2, NZ - 1, 16, 128), BF16),
            pltpu.VMEM((2, NY, 16, 128), BF16),
            dma((6,)),
            dma((8,)),
            dma((8, 24)), dma((8, 24)),
            dma((4, 3)), dma((4, 3)),
            dma((9,)), dma((9,)),
            dma((2, 29)), dma((2, 29)),
        ],
        compiler_params=pltpu.CompilerParams(
            collective_id=0, has_side_effects=True, vmem_limit_bytes=56 * 1024 * 1024
        ),
        name="window_blocks",
    )(
        tokens, grad_out, first_gain[None], second_gain[None],
        first_qkv_weight, first_out_weight, second_qkv_weight, second_out_weight,
        first_bias.T, second_bias.T, rel_index, classes,
    )


def solution(mesh):
    tile = P("rep", "lat", "lon", None)
    rows = P(("lat", "lon"), None)
    in_specs = (tile, tile, P(), rows, rows, P(), P(), rows, rows, P(), P(), P("lat", "lon"))
    return jax.shard_map(
        on_device, mesh=mesh, in_specs=in_specs, out_specs=(tile, rows, rows), check_vma=False
    )
```
